32 devices in a mesh: ctx: 4 (over z), head: 4 (over x, core), band: 2 (over y).
Axes of the slice: x: 2, y: 2, z: 4, core: 2. Of those that a mesh axis runs over, the one named last changes fastest.
Arguments:
- queries: bfloat16 [8192, 1024], P(('band', 'ctx', 'head')), parts along dimension 0, may hold values from -6 to 6
- key_states: bfloat16 [8192, 1024], P(('band', 'ctx', 'head')), parts along dimension 0, may hold values from -6 to 6
- value_states: bfloat16 [8192, 1024], P(('band', 'ctx', 'head')), parts along dimension 0, may hold values from -6 to 6
- grad_output: bfloat16 [8192, 1024], P(('band', 'ctx', 'head')), parts along dimension 0, may hold values from -24 to 24
- block_slot: int32 [128], P('band'), parts along dimension 0, may hold values from 0 to 63, as said below
- neighbours: int32 [128, 8], P('band'), parts along dimension 0, may hold values from 0 to 63, as said below
Outputs:
- grad_queries: bfloat16 [8192, 1024], P(('band', 'ctx', 'head')), parts along dimension 0
- grad_keys: bfloat16 [8192, 1024], P(('band', 'ctx', 'head')), parts along dimension 0
- grad_values: bfloat16 [8192, 1024], P(('band', 'ctx', 'head')), parts along dimension 0
The draws below stay inside these ranges and needn't reach their ends.
There are 2 independent parts, one for each index of `band`. The reference program is written for one: setup_inputs(seed, part) draws one part's arguments, and reference() takes and returns one part's arrays. A program takes and returns all parts, laid end to end along the dimension named above; each array names one. Nothing has to cross between parts.
Inputs may be any that keep to these rules, and one draw needn't show every extreme that they name: `block_slot`: a permutation of the 64 slots. `neighbours`: entry 0 of row b is b. The slot of every other entry lies on a ctx index, slot // 16, at most 1 away cyclically from that of b. These entries are distinct where at least 7 such blocks exist, and else repeat.
All inputs are finite; a program needn't handle non-finite values.
Results may differ from the reference program's by a relative error of at most 0.0088.
Values may be sent and summed in bfloat16 or wider, within the bound.
No kernel may reach another device: no remote copies, remote signals or barrier semaphores. Data moves between devices by JAX's collectives and lax.ppermute only.
A program may use at most 128 MiB of HBM per device.

```python
import jax
import jax.numpy as jnp
from jax import lax

HEADS = 16
HEAD_DIM = 64
D = 1024
BLOCK_TOK = 64
NBR = 8
REACH = 1
BLK_DEV = 16
BLOCKS = 64
TOKENS = 4096


def layout_draw(key):
    per_device = BLK_DEV
    dev_count = BLOCKS // BLK_DEV
    rotation = jax.random.randint(jax.random.fold_in(key, 11), (), 0, dev_count)
    inner_scores = jax.random.randint(jax.random.fold_in(key, 12), (dev_count, per_device), 0, 1 << 20)
    inner_order = jnp.argsort(inner_scores * per_device + jnp.arange(per_device)[None, :], axis=1)
    sphere = jnp.arange(BLOCKS, dtype=jnp.int32)
    home_dev = (sphere // per_device + rotation) % dev_count
    slot_of = (home_dev * per_device + inner_order[sphere // per_device, sphere % per_device]).astype(jnp.int32)
    sphere_of = jnp.zeros((BLOCKS,), jnp.int32).at[slot_of].set(sphere)
    deltas = sorted(set((offset % dev_count for offset in range(-REACH, REACH + 1))))
    delta_table = jnp.array(deltas, dtype=jnp.int32)
    cand_count = len(deltas) * per_device
    candidates = (home_dev[:, None, None] + delta_table[None, :, None]) % dev_count * per_device
    candidates = (candidates + jnp.arange(per_device, dtype=jnp.int32)[None, None, :]).reshape(BLOCKS, cand_count)
    draw_scores = jax.random.randint(jax.random.fold_in(key, 13), (BLOCKS, cand_count), 0, 1 << 20)
    draw_scores = draw_scores * cand_count + jnp.arange(cand_count)[None, :]
    draw_scores = jnp.where(candidates == slot_of[:, None], -1, draw_scores)
    ranking = jnp.argsort(-draw_scores, axis=1)[:, :cand_count - 1]
    picked = ranking[:, jnp.arange(NBR - 1) % (cand_count - 1)]
    chosen_slots = jnp.take_along_axis(candidates, picked, axis=1)
    neighbour_rows = jnp.concatenate([sphere[:, None], sphere_of[chosen_slots]], axis=1)
    return (slot_of, neighbour_rows.astype(jnp.int32))


def draw_block_slot(key, part):
    return layout_draw(key)[0]


def draw_neighbours(key, part):
    return layout_draw(key)[1]


def draw_queries(key, part):
    return jnp.clip(jax.random.normal(jax.random.fold_in(key, 23), (TOKENS, D), jnp.float32), -6.0, 6.0).astype(jnp.bfloat16)


def draw_key_states(key, part):
    return jnp.clip(jax.random.normal(jax.random.fold_in(key, 24), (TOKENS, D), jnp.float32), -6.0, 6.0).astype(jnp.bfloat16)


def block_levels(key, shape, cuts, least, top_value):
    factor_of = 1.0
    for position, parts in cuts:
        steps = jax.random.uniform(jax.random.fold_in(jax.random.fold_in(key, 6), position), (parts,), jnp.float32, least / len(cuts), top_value / len(cuts))
        factor_of = factor_of * jnp.repeat(jnp.exp(steps), shape[position] // parts).reshape((-1,) + (1,) * (len(shape) - 1 - position))
    return factor_of


def centred(key, extent, scale, reach, pieces=(), kind=jnp.bfloat16):
    entries = jax.random.normal(key, extent, jnp.float32) * scale
    if len(pieces) > 0:
        entries = block_levels(key, extent, pieces, -0.22, 0.18) * entries
    return jnp.clip(entries, min=-reach, max=reach).astype(kind)


def setup_inputs(seed: int = 0, part: int = 0) -> dict:
    splits = jax.random.split(jax.random.key(seed), 7)
    part_keys = jax.random.split(jax.random.fold_in(splits[6], part), 7)
    queries = draw_queries(jax.random.fold_in(jax.random.fold_in(splits[6], part), 71), part)
    key_states = draw_key_states(jax.random.fold_in(jax.random.fold_in(splits[6], part), 71), part)
    value_states = centred(part_keys[2], (TOKENS, D), 1.0, 6.0, ((0, 16),))
    grad_output = jnp.clip(jax.random.uniform(part_keys[3], (TOKENS, D), jnp.float32, -24.0, 24.0) * block_levels(part_keys[3], (TOKENS, D), ((0, 16),), -0.4, 0.0), -24.0, 24.0).astype(jnp.bfloat16)
    block_slot = draw_block_slot(jax.random.fold_in(jax.random.fold_in(splits[6], part), 71), part)
    neighbours = draw_neighbours(jax.random.fold_in(jax.random.fold_in(splits[6], part), 71), part)
    return dict(queries=queries, key_states=key_states, value_states=value_states, grad_output=grad_output, block_slot=block_slot, neighbours=neighbours)


def reference(queries, key_states, value_states, grad_output, block_slot, neighbours):
    softmax_scale = HEAD_DIM ** -0.5
    slot_ids = jnp.arange(BLOCKS, dtype=jnp.int32)
    sphere_of = jnp.zeros((BLOCKS,), jnp.int32).at[block_slot].set(slot_ids)
    listed = block_slot[neighbours[sphere_of]].astype(jnp.int32)
    block_shape = (BLOCKS, BLOCK_TOK, HEADS, HEAD_DIM)
    query_blocks = queries.reshape(block_shape)
    key_blocks = key_states.reshape(block_shape)
    value_blocks = value_states.reshape(block_shape)
    grad_blocks = grad_output.reshape(block_shape)

    def one_slot(carried, slot_now):
        grad_key_acc, grad_val_acc = carried
        chosen = listed[slot_now]
        query_now = query_blocks[slot_now].astype(jnp.float32)
        grad_now = grad_blocks[slot_now].astype(jnp.float32)
        key_now = key_blocks[chosen].reshape(NBR * BLOCK_TOK, HEADS, HEAD_DIM).astype(jnp.float32)
        value_now = value_blocks[chosen].reshape(NBR * BLOCK_TOK, HEADS, HEAD_DIM).astype(jnp.float32)
        scores = jnp.einsum("qhd,khd->hqk", query_now, key_now) * softmax_scale
        probability = jax.nn.softmax(scores, axis=-1)
        grad_prob = jnp.einsum("qhd,khd->hqk", grad_now, value_now)
        row_delta = jnp.sum(probability * grad_prob, axis=-1, keepdims=True)
        grad_score = probability * (grad_prob - row_delta)
        prob_low = lax.optimization_barrier(probability.astype(jnp.bfloat16)).astype(jnp.float32)
        score_low = lax.optimization_barrier(grad_score.astype(jnp.bfloat16)).astype(jnp.float32)
        value_part = jnp.einsum("hqk,qhd->khd", prob_low, grad_now)
        key_part = jnp.einsum("hqk,qhd->khd", score_low, query_now) * softmax_scale
        query_grad = (jnp.einsum("hqk,khd->qhd", score_low, key_now) * softmax_scale).astype(jnp.bfloat16)
        grad_key_acc = grad_key_acc.at[chosen].add(key_part.reshape(NBR, BLOCK_TOK, HEADS, HEAD_DIM))
        grad_val_acc = grad_val_acc.at[chosen].add(value_part.reshape(NBR, BLOCK_TOK, HEADS, HEAD_DIM))
        return (grad_key_acc, grad_val_acc), query_grad

    start = (jnp.zeros(block_shape, jnp.float32), jnp.zeros(block_shape, jnp.float32))
    (grad_key_acc, grad_val_acc), query_grads = lax.scan(one_slot, start, slot_ids)
    grad_queries = query_grads.reshape(TOKENS, D)
    grad_keys = grad_key_acc.reshape(TOKENS, D).astype(jnp.bfloat16)
    grad_values = grad_val_acc.reshape(TOKENS, D).astype(jnp.bfloat16)
    return (grad_queries, grad_keys, grad_values)
```

```python
import functools
import math

import jax
import jax.numpy as jnp
from jax import lax
from jax.experimental import pallas as pl
from jax.experimental.pallas import tpu as pltpu
from jax.sharding import PartitionSpec as P

HEAD_DIM = 64
BLOCK_TOK = 64
NBR = 8
REACH = 1
PAIR = 2 * HEAD_DIM
LIST_ROWS = NBR * BLOCK_TOK
SCALE = HEAD_DIM ** -0.5
EXP2_SCALE = SCALE * math.log2(math.e)
VMEM_LIMIT = 48 * 1024 * 1024


def from_behind(value, axis, steps):
    count = lax.axis_size(axis)
    pairs = [(source, (source + steps) % count) for source in range(count)]
    return lax.ppermute(value, axis, pairs)


def call_kernel(kernel, out_shape, in_memory, scratch_shapes=(), **cost):
    outs = jax.tree.map(lambda _: pl.BlockSpec(memory_space=pltpu.VMEM), out_shape)
    return pl.pallas_call(
        kernel,
        out_shape=out_shape,
        in_specs=[pl.BlockSpec(memory_space=space) for space in in_memory],
        out_specs=outs,
        scratch_shapes=list(scratch_shapes),
        compiler_params=pltpu.CompilerParams(vmem_limit_bytes=VMEM_LIMIT),
        cost_estimate=pl.CostEstimate(**cost) if cost else None,
    )


def columns_of(ref, head):
    return ref[:, head * HEAD_DIM : (head + 1) * HEAD_DIM]


def pack_kernel(query_ref, grad_ref, key_ref, value_ref, out_ref):
    rows = query_ref.shape[0]
    for head in range(out_ref.shape[0]):
        out_ref[head, :rows] = jnp.concatenate(
            [columns_of(query_ref, head), columns_of(grad_ref, head)], axis=1
        )
        out_ref[head, rows:] = jnp.concatenate(
            [columns_of(key_ref, head), columns_of(value_ref, head)], axis=1
        )


def unpack_kernel(packed_ref, query_ref, key_ref, value_ref):
    rows = query_ref.shape[0]
    half = rows // 2
    for pair in range(packed_ref.shape[0] // 2):
        lanes = slice(pair * PAIR, (pair + 1) * PAIR)
        even, odd = packed_ref[2 * pair], packed_ref[2 * pair + 1]
        key_ref[:, lanes] = jnp.concatenate([even[:rows, :HEAD_DIM], odd[:rows, :HEAD_DIM]], axis=1)
        value_ref[:, lanes] = jnp.concatenate([even[:rows, HEAD_DIM:], odd[:rows, HEAD_DIM:]], axis=1)
        query_ref[:half, lanes] = jnp.concatenate([even[rows:, :HEAD_DIM], odd[rows:, :HEAD_DIM]], axis=1)
        query_ref[half:, lanes] = jnp.concatenate([even[rows:, HEAD_DIM:], odd[rows:, HEAD_DIM:]], axis=1)


def block_pair_gradients(rows_a, rows_b, list_a, list_b):
    low = lax.broadcasted_iota(jnp.int32, (BLOCK_TOK, PAIR), 1) < HEAD_DIM
    zero = jnp.zeros_like(rows_a)
    diagonal = jnp.concatenate(
        [
            jnp.concatenate([jnp.where(low, rows_a, zero), zero], axis=1),
            jnp.concatenate([zero, jnp.where(low, rows_b, zero)], axis=1),
            jnp.concatenate([jnp.where(low, zero, rows_a), zero], axis=1),
            jnp.concatenate([zero, jnp.where(low, zero, rows_b)], axis=1),
        ],
        axis=0,
    )
    listed = jnp.concatenate([list_a, list_b], axis=1)
    both = lax.dot_general(listed, diagonal, (((1,), (1,)), ((), ())), preferred_element_type=jnp.float32)
    scores, grad_prob = both[:, :PAIR], both[:, PAIR:]
    top = jnp.max(scores, axis=0, keepdims=True)
    weights = jnp.exp2((scores - top) * EXP2_SCALE)
    inverse = 1.0 / jnp.sum(weights, axis=0, keepdims=True)
    row_delta = jnp.sum(weights * grad_prob, axis=0, keepdims=True) * inverse
    probability = weights * inverse
    score_low = (probability * (grad_prob - row_delta)).astype(jnp.bfloat16)
    prob_low = probability.astype(jnp.bfloat16)
    grad_listed = lax.dot_general(
        jnp.concatenate([score_low, prob_low], axis=1),
        diagonal,
        (((1,), (0,)), ((), ())),
        preferred_element_type=jnp.float32,
    )
    grad_query = lax.dot_general(
        score_low, listed, (((0,), (0,)), ((), ())), preferred_element_type=jnp.float32
    )
    return grad_query[:BLOCK_TOK, :PAIR], grad_query[BLOCK_TOK:, PAIR:], grad_listed


def accumulate_blocks(table_ref, nbr_ref, query_rows, key_value_rows, grad_query_ref, acc_ref):
    def gather_list(block):
        picks = [table_ref[nbr_ref[block, n]] for n in range(NBR)]
        return picks, jnp.concatenate([key_value_rows(pick) for pick in picks], axis=0)

    def step(index, carry):
        slot_a, slot_b = table_ref[2 * index], table_ref[2 * index + 1]
        picks_a, list_a = gather_list(2 * index)
        picks_b, list_b = gather_list(2 * index + 1)
        grad_a, grad_b, grad_listed = block_pair_gradients(
            query_rows(slot_a), query_rows(slot_b), list_a, list_b
        )
        grad_query_ref[slot_a] = grad_a * SCALE
        grad_query_ref[slot_b] = grad_b * SCALE
        for n in range(NBR):
            part = slice(n * BLOCK_TOK, (n + 1) * BLOCK_TOK)
            acc_ref[picks_a[n]] += grad_listed[part, :PAIR]
            acc_ref[picks_b[n]] += grad_listed[part, PAIR:]
        return carry

    acc_ref[...] = jnp.zeros_like(acc_ref)
    lax.fori_loop(0, nbr_ref.shape[0] // 2, step, 0)


def key_scale():
    low = lax.broadcasted_iota(jnp.int32, (1, PAIR), 1) < HEAD_DIM
    return jnp.where(low, jnp.float32(SCALE), jnp.float32(1.0))


def head_kernel(table_ref, nbr_ref, packed_ref, out_ref, grad_query_ref, acc_ref):
    sources, double_rows, _ = packed_ref.shape
    rows = double_rows // 2
    half = rows // 2
    per_source = rows // BLOCK_TOK

    def block_rows(first, slot):
        start = pl.multiple_of(first + slot % per_source * BLOCK_TOK, BLOCK_TOK)
        return packed_ref[slot // per_source, pl.ds(start, BLOCK_TOK)]

    accumulate_blocks(
        table_ref,
        nbr_ref,
        functools.partial(block_rows, 0),
        functools.partial(block_rows, rows),
        grad_query_ref,
        acc_ref,
    )

    def write(source, carry):
        for place in range(per_source):
            slot = source * per_source + place
            out_ref[source, place * BLOCK_TOK : (place + 1) * BLOCK_TOK] = (
                acc_ref[slot] * key_scale()
            ).astype(jnp.bfloat16)
        for place in range(per_source // 2):
            slot = source * per_source + place
            both = jnp.concatenate(
                [grad_query_ref[slot][:, :HEAD_DIM], grad_query_ref[slot + per_source // 2][:, :HEAD_DIM]],
                axis=1,
            )
            start = rows + place * BLOCK_TOK
            out_ref[source, start : start + BLOCK_TOK] = both.astype(jnp.bfloat16)
        return carry

    lax.fori_loop(0, sources, write, 0)


def one_head_each(queries, key_states, value_states, grad_output, block_slot, neighbours):
    axes = ("ctx", "head")
    rows, width = queries.shape
    heads = width // HEAD_DIM
    blocks = block_slot.shape[0]
    in_vmem, in_smem = pltpu.VMEM, pltpu.SMEM
    packed = call_kernel(
        pack_kernel,
        jax.ShapeDtypeStruct((heads, 2 * rows, PAIR), jnp.bfloat16),
        [in_vmem] * 4,
    )(queries, grad_output, key_states, value_states)
    packed = lax.all_to_all(packed, axes, split_axis=0, concat_axis=0, tiled=True)
    grads = call_kernel(
        head_kernel,
        jax.ShapeDtypeStruct((heads, 3 * rows // 2, PAIR), jnp.bfloat16),
        [in_smem, in_smem, in_vmem],
        [pltpu.VMEM((blocks, BLOCK_TOK, PAIR), jnp.float32)] * 2,
        flops=10 * blocks * BLOCK_TOK * LIST_ROWS * HEAD_DIM,
        bytes_accessed=7 * heads * rows * PAIR,
        transcendentals=blocks * BLOCK_TOK * LIST_ROWS,
    )(block_slot, neighbours, packed)
    grads = lax.all_to_all(grads, axes, split_axis=0, concat_axis=0, tiled=True)
    return call_kernel(
        unpack_kernel,
        (jax.ShapeDtypeStruct((rows, width), jnp.bfloat16),) * 3,
        [in_vmem],
    )(grads)


def halo_kernel(table_ref, nbr_ref, query_ref, key_value_ref, grad_query_out, acc_out, grad_query_ref, acc_ref):
    for head in range(query_ref.shape[0]):
        accumulate_blocks(
            table_ref,
            nbr_ref,
            lambda slot: query_ref[head, slot],
            lambda slot: key_value_ref[head, slot],
            grad_query_ref,
            acc_ref,
        )
        grad_query_out[head] = grad_query_ref[...]
        acc_out[head] = acc_ref[...] * key_scale()


def halo_exchange(queries, key_states, value_states, grad_output, block_slot, neighbours):
    def to_heads(value):
        return lax.all_to_all(value, "head", split_axis=1, concat_axis=0, tiled=True)

    def paired(left, right):
        parts = [to_heads(x).reshape(-1, BLOCK_TOK, heads, 1, HEAD_DIM) for x in (left, right)]
        both = jnp.concatenate(parts, axis=3)
        return jnp.moveaxis(both, 2, 0).reshape(heads, -1, BLOCK_TOK, PAIR)

    heads = queries.shape[1] // HEAD_DIM // lax.axis_size("head")
    query_side = paired(queries, grad_output)
    key_side = paired(key_states, value_states)
    blocks = query_side.shape[1]
    ctx_size = lax.axis_size("ctx")
    ctx_here = lax.axis_index("ctx")
    slot_ids = jnp.arange(block_slot.shape[0], dtype=jnp.int32)
    matches = (block_slot[None, :] == slot_ids[:, None]).astype(jnp.int32)
    sphere_of = jnp.sum(matches * slot_ids[None, :], axis=1)
    my_slots = ctx_here * blocks + jnp.arange(blocks, dtype=jnp.int32)
    listed = block_slot[neighbours[sphere_of[my_slots]]]
    gap = (listed // blocks - ctx_here + ctx_size + REACH) % ctx_size - REACH
    lookup = (gap + REACH) * blocks + listed % blocks
    offsets = range(-REACH, REACH + 1)
    span = jnp.concatenate(
        [key_side if o == 0 else from_behind(key_side, "ctx", -o) for o in offsets], axis=1
    )
    span_blocks = span.shape[1]
    grad_query, partial = call_kernel(
        halo_kernel,
        (
            jax.ShapeDtypeStruct((heads, blocks, BLOCK_TOK, PAIR), jnp.float32),
            jax.ShapeDtypeStruct((heads, span_blocks, BLOCK_TOK, PAIR), jnp.float32),
        ),
        [pltpu.SMEM, pltpu.SMEM, pltpu.VMEM, pltpu.VMEM],
        [
            pltpu.VMEM((blocks, BLOCK_TOK, PAIR), jnp.float32),
            pltpu.VMEM((span_blocks, BLOCK_TOK, PAIR), jnp.float32),
        ],
    )(jnp.arange(span_blocks, dtype=jnp.int32), lookup.astype(jnp.int32), query_side, span)
    returned = partial.reshape(heads, 2 * REACH + 1, blocks, BLOCK_TOK, PAIR)
    summed = returned[:, REACH]
    for offset in offsets:
        if offset != 0:
            summed = summed + from_behind(returned[:, offset + REACH], "ctx", offset)

    def to_tokens(value):
        value = jnp.moveaxis(value.astype(jnp.bfloat16), 0, 2).reshape(-1, heads * HEAD_DIM)
        return lax.all_to_all(value, "head", split_axis=0, concat_axis=1, tiled=True)

    return (
        to_tokens(grad_query[..., :HEAD_DIM]),
        to_tokens(summed[..., :HEAD_DIM]),
        to_tokens(summed[..., HEAD_DIM:]),
    )


def solution(mesh):
    devices = mesh.shape["ctx"] * mesh.shape["head"]

    def body(queries, *rest):
        rows, width = queries.shape
        one_each = width == devices * HEAD_DIM and rows % (2 * BLOCK_TOK) == 0
        return (one_head_each if one_each else halo_exchange)(queries, *rest)

    tokens = P(("band", "ctx", "head"), None)
    return jax.shard_map(
        body,
        mesh=mesh,
        in_specs=(tokens,) * 4 + (P("band"), P("band", None)),
        out_specs=(tokens,) * 3,
        check_vma=False,
    )
```

```python
import math

import jax
import jax.numpy as jnp
from jax import lax
from jax.experimental import pallas as pl
from jax.experimental.pallas import tpu as pltpu
from jax.sharding import PartitionSpec as P

HEAD_DIM = 64
BLOCK_TOK = 64
NBR = 8
REACH = 1
PAIR = 2 * HEAD_DIM
LIST_ROWS = NBR * BLOCK_TOK
SCALE = HEAD_DIM ** -0.5
EXP2_SCALE = SCALE * math.log2(math.e)
SUBLANES = 8
CHUNK = 16
VMEM_LIMIT = 48 * 1024 * 1024
PACK_VMEM_LIMIT = 60 * 1024 * 1024
NT = (((1,), (1,)), ((), ()))
NN = (((1,), (0,)), ((), ()))
TN = (((0,), (0,)), ((), ()))


def from_behind(value, axis, steps):
    count = lax.axis_size(axis)
    pairs = [(source, (source + steps) % count) for source in range(count)]
    return lax.ppermute(value, axis, pairs)


def call_kernel(kernel, out_shape, in_memory, scratch_shapes=(), **cost):
    outs = jax.tree.map(lambda _: pl.BlockSpec(memory_space=pltpu.VMEM), out_shape)
    return pl.pallas_call(
        kernel,
        out_shape=out_shape,
        in_specs=[pl.BlockSpec(memory_space=space) for space in in_memory],
        out_specs=outs,
        scratch_shapes=list(scratch_shapes),
        compiler_params=pltpu.CompilerParams(vmem_limit_bytes=VMEM_LIMIT),
        cost_estimate=pl.CostEstimate(**cost) if cost else None,
    )


def columns_of(ref, head):
    return ref[:, head * HEAD_DIM : (head + 1) * HEAD_DIM]


def pack_kernel(query_ref, grad_ref, key_ref, value_ref, out_ref):
    for head in range(out_ref.shape[0]):
        out_ref[head, 0] = jnp.concatenate([columns_of(query_ref, head), columns_of(grad_ref, head)], axis=1)
        out_ref[head, 1] = jnp.concatenate([columns_of(key_ref, head), columns_of(value_ref, head)], axis=1)


def unpack_kernel(packed_ref, query_ref, key_ref, value_ref):
    rows = query_ref.shape[0]
    for pair in range(packed_ref.shape[0] // 2):
        lanes = slice(pair * PAIR, (pair + 1) * PAIR)
        even, odd = packed_ref[2 * pair], packed_ref[2 * pair + 1]
        key_ref[:, lanes] = jnp.concatenate([even[:rows, :HEAD_DIM], odd[:rows, :HEAD_DIM]], axis=1)
        value_ref[:, lanes] = jnp.concatenate([even[:rows, HEAD_DIM:], odd[:rows, HEAD_DIM:]], axis=1)
        for place in range(rows // (2 * BLOCK_TOK)):
            start = rows + place * BLOCK_TOK
            part = slice(start, start + BLOCK_TOK)
            first = slice(2 * place * BLOCK_TOK, (2 * place + 1) * BLOCK_TOK)
            second = slice((2 * place + 1) * BLOCK_TOK, (2 * place + 2) * BLOCK_TOK)
            query_ref[first, lanes] = jnp.concatenate([even[part, :HEAD_DIM], odd[part, :HEAD_DIM]], axis=1)
            query_ref[second, lanes] = jnp.concatenate([even[part, HEAD_DIM:], odd[part, HEAD_DIM:]], axis=1)


def diagonal_of(rows):
    low = lax.broadcasted_iota(jnp.int32, (BLOCK_TOK, PAIR), 1) < HEAD_DIM
    rows_a, rows_b = rows[:BLOCK_TOK], rows[BLOCK_TOK:]
    zero = jnp.zeros_like(rows_a)
    return jnp.concatenate(
        [
            jnp.concatenate([jnp.where(low, rows_a, zero), zero], axis=1),
            jnp.concatenate([zero, jnp.where(low, rows_b, zero)], axis=1),
            jnp.concatenate([jnp.where(low, zero, rows_a), zero], axis=1),
            jnp.concatenate([zero, jnp.where(low, zero, rows_b)], axis=1),
        ],
        axis=0,
    )


def fold_rows(value, reduce):
    return reduce(value.reshape(-1, SUBLANES, PAIR), axis=0)


def accumulate_blocks(pairs, list_ref, place_ref, query_pair, key_value_rows, write_query, acc_ref, buffers):
    count = 2 * NBR

    def listed_of(pair):
        starts = [pl.multiple_of(list_ref[pair * count + n], BLOCK_TOK) for n in range(count)]
        blocks = [key_value_rows(start) for start in starts]
        return jnp.concatenate(
            [jnp.concatenate(blocks[:NBR], axis=0), jnp.concatenate(blocks[NBR:], axis=0)], axis=1
        )

    def scores_stage(pair, buffer):
        both_ref, _ = buffer
        both_ref[...] = lax.dot_general(
            listed_of(pair), diagonal_of(query_pair(pair)), NT, preferred_element_type=jnp.float32
        )

    def softmax_stage(buffer):
        both_ref, low_ref = buffer
        chunks = [slice(start, start + CHUNK) for start in range(0, LIST_ROWS, CHUNK)]
        top = None
        for rows in chunks:
            part = fold_rows(both_ref[rows, :PAIR], jnp.max)
            top = part if top is None else jnp.maximum(top, part)
        top = jnp.max(top, axis=0, keepdims=True) * EXP2_SCALE
        total = delta = None
        for rows in chunks:
            weights = jnp.exp2(both_ref[rows, :PAIR] * EXP2_SCALE - top)
            part, part_delta = fold_rows(weights, jnp.sum), fold_rows(weights * both_ref[rows, PAIR:], jnp.sum)
            both_ref[rows, :PAIR] = weights
            total = part if total is None else total + part
            delta = part_delta if delta is None else delta + part_delta
        inverse = 1.0 / jnp.sum(total, axis=0, keepdims=True)
        row_delta = jnp.sum(delta, axis=0, keepdims=True) * inverse
        for rows in chunks:
            probability = both_ref[rows, :PAIR] * inverse
            grad_score = probability * (both_ref[rows, PAIR:] - row_delta)
            low_ref[rows, :PAIR] = grad_score.astype(jnp.bfloat16)
            low_ref[rows, PAIR:] = probability.astype(jnp.bfloat16)

    def gradients_stage(pair, buffer):
        _, low_ref = buffer
        grad_listed = lax.dot_general(
            low_ref[...], diagonal_of(query_pair(pair)), NN, preferred_element_type=jnp.float32
        )
        for n in range(NBR):
            for side in range(2):
                start = pl.multiple_of(place_ref[pair * count + side * NBR + n], BLOCK_TOK)
                acc_ref[pl.ds(start, BLOCK_TOK)] += grad_listed[
                    n * BLOCK_TOK : (n + 1) * BLOCK_TOK, side * PAIR : (side + 1) * PAIR
                ]
        grad_query = lax.dot_general(
            low_ref[:, :PAIR], listed_of(pair), TN, preferred_element_type=jnp.float32
        )
        write_query(
            pair,
            jnp.concatenate(
                [grad_query[:BLOCK_TOK, :HEAD_DIM], grad_query[BLOCK_TOK:, PAIR : PAIR + HEAD_DIM]], axis=1
            )
            * SCALE,
        )

    even, odd = buffers[:2], buffers[2:]
    last = pairs - 1
    acc_ref[...] = jnp.zeros_like(acc_ref)
    scores_stage(0, even)
    softmax_stage(even)
    scores_stage(1, odd)

    def step(index, carry):
        pair = 2 * index
        gradients_stage(pair, even)
        softmax_stage(odd)
        scores_stage(jnp.minimum(pair + 2, last), even)
        gradients_stage(pair + 1, odd)
        softmax_stage(even)
        scores_stage(jnp.minimum(pair + 3, last), odd)
        return carry

    lax.fori_loop(0, pairs // 2, step, 0)


def key_scale():
    low = lax.broadcasted_iota(jnp.int32, (1, PAIR), 1) < HEAD_DIM
    return jnp.where(low, jnp.float32(SCALE), jnp.float32(1.0))


def head_kernel(list_ref, place_ref, packed_ref, out_ref, acc_ref, *buffers):
    sources, out_rows, _ = out_ref.shape
    rows = 2 * out_rows // 3
    pairs_each = rows // (2 * BLOCK_TOK)

    def query_pair(pair):
        start = pair // pairs_each * (2 * rows) + pair % pairs_each * (2 * BLOCK_TOK)
        return packed_ref[pl.ds(pl.multiple_of(start, 2 * BLOCK_TOK), 2 * BLOCK_TOK)]

    def write_query(pair, value):
        start = rows + pl.multiple_of(pair % pairs_each * BLOCK_TOK, BLOCK_TOK)
        out_ref[pair // pairs_each, pl.ds(start, BLOCK_TOK)] = value.astype(jnp.bfloat16)

    accumulate_blocks(
        sources * pairs_each,
        list_ref,
        place_ref,
        query_pair,
        lambda start: packed_ref[pl.ds(start, BLOCK_TOK)],
        write_query,
        acc_ref,
        buffers,
    )

    def write(source, carry):
        start = pl.multiple_of(source * rows, rows)
        out_ref[source, :rows] = (acc_ref[pl.ds(start, rows)] * key_scale()).astype(jnp.bfloat16)
        return carry

    lax.fori_loop(0, sources, write, 0)


def work_buffers():
    return [
        pltpu.VMEM((LIST_ROWS, 2 * PAIR), jnp.float32),
        pltpu.VMEM((LIST_ROWS, 2 * PAIR), jnp.bfloat16),
    ] * 2


def listed_slots(block_slot, neighbours):
    slot_ids = jnp.arange(block_slot.shape[0], dtype=jnp.int32)
    matches = (block_slot[None, :] == slot_ids[:, None]).astype(jnp.int32)
    sphere_of = jnp.sum(matches * slot_ids[None, :], axis=1)
    return block_slot[neighbours[sphere_of]]


def one_head_each(queries, key_states, value_states, grad_output, block_slot, neighbours):
    axes = ("ctx", "head")
    rows, width = queries.shape
    heads = width // HEAD_DIM
    tokens = heads * rows
    in_vmem, in_smem = pltpu.VMEM, pltpu.SMEM
    packed = pl.pallas_call(
        pack_kernel,
        grid=(2,),
        in_specs=[pl.BlockSpec((rows // 2, width), lambda i: (i, 0))] * 4,
        out_specs=pl.BlockSpec((heads, 2, rows // 2, PAIR), lambda i: (0, 0, i, 0)),
        out_shape=jax.ShapeDtypeStruct((heads, 2, rows, PAIR), jnp.bfloat16),
        compiler_params=pltpu.CompilerParams(vmem_limit_bytes=PACK_VMEM_LIMIT),
    )(queries, grad_output, key_states, value_states)
    packed = lax.all_to_all(packed, axes, split_axis=0, concat_axis=0, tiled=True)
    place = listed_slots(block_slot, neighbours).reshape(-1) * BLOCK_TOK
    start = place // rows * (2 * rows) + rows + place % rows
    grads = call_kernel(
        head_kernel,
        jax.ShapeDtypeStruct((heads, 3 * rows // 2, PAIR), jnp.bfloat16),
        [in_smem, in_smem, in_vmem],
        [pltpu.VMEM((tokens, PAIR), jnp.float32)] + work_buffers(),
        flops=10 * tokens * LIST_ROWS * HEAD_DIM,
        bytes_accessed=7 * tokens * PAIR,
        transcendentals=tokens * LIST_ROWS,
    )(start, place, packed.reshape(2 * tokens, PAIR))
    grads = lax.all_to_all(grads, axes, split_axis=0, concat_axis=0, tiled=True)
    return call_kernel(
        unpack_kernel,
        (jax.ShapeDtypeStruct((rows, width), jnp.bfloat16),) * 3,
        [in_vmem],
    )(grads)


def halo_kernel(list_ref, query_ref, key_value_ref, grad_query_out, acc_out, *buffers):
    for head in range(query_ref.shape[0]):

        def write_query(pair, value):
            grad_query_out[head, pl.ds(pl.multiple_of(pair * BLOCK_TOK, BLOCK_TOK), BLOCK_TOK)] = value

        accumulate_blocks(
            query_ref.shape[1] // (2 * BLOCK_TOK),
            list_ref,
            list_ref,
            lambda pair: query_ref[head, pl.ds(pl.multiple_of(pair * 2 * BLOCK_TOK, 2 * BLOCK_TOK), 2 * BLOCK_TOK)],
            lambda start: key_value_ref[head, pl.ds(start, BLOCK_TOK)],
            write_query,
            acc_out.at[head],
            buffers,
        )
        acc_out[head] = acc_out[head] * key_scale()


def halo_exchange(queries, key_states, value_states, grad_output, block_slot, neighbours):
    def to_heads(value):
        return lax.all_to_all(value, "head", split_axis=1, concat_axis=0, tiled=True)

    def paired(left, right):
        parts = [to_heads(x).reshape(-1, heads, 1, HEAD_DIM) for x in (left, right)]
        both = jnp.concatenate(parts, axis=2)
        return jnp.moveaxis(both, 1, 0).reshape(heads, -1, PAIR)

    heads = queries.shape[1] // HEAD_DIM // lax.axis_size("head")
    query_side = paired(queries, grad_output)
    key_side = paired(key_states, value_states)
    rows = query_side.shape[1]
    blocks = rows // BLOCK_TOK
    ctx_size = lax.axis_size("ctx")
    ctx_here = lax.axis_index("ctx")
    listed = lax.dynamic_slice_in_dim(listed_slots(block_slot, neighbours), ctx_here * blocks, blocks, 0)
    gap = (listed // blocks - ctx_here + ctx_size + REACH) % ctx_size - REACH
    lookup = (gap + REACH) * blocks + listed % blocks
    offsets = range(-REACH, REACH + 1)
    span = jnp.concatenate(
        [key_side if o == 0 else from_behind(key_side, "ctx", -o) for o in offsets], axis=1
    )
    grad_query, partial = call_kernel(
        halo_kernel,
        (
            jax.ShapeDtypeStruct((heads, rows // 2, PAIR), jnp.float32),
            jax.ShapeDtypeStruct(span.shape, jnp.float32),
        ),
        [pltpu.SMEM, pltpu.VMEM, pltpu.VMEM],
        work_buffers(),
    )(lookup.reshape(-1) * BLOCK_TOK, query_side, span)
    returned = partial.reshape(heads, 2 * REACH + 1, rows, PAIR)
    summed = returned[:, REACH]
    for offset in offsets:
        if offset != 0:
            summed = summed + from_behind(returned[:, offset + REACH], "ctx", offset)

    def to_tokens(value):
        value = jnp.moveaxis(value.astype(jnp.bfloat16), 0, 1).reshape(rows, heads * HEAD_DIM)
        return lax.all_to_all(value, "head", split_axis=0, concat_axis=1, tiled=True)

    grad_query = grad_query.reshape(heads, blocks // 2, BLOCK_TOK, 2, HEAD_DIM)
    return (
        to_tokens(jnp.swapaxes(grad_query, 2, 3).reshape(heads, rows, HEAD_DIM)),
        to_tokens(summed[..., :HEAD_DIM]),
        to_tokens(summed[..., HEAD_DIM:]),
    )


def solution(mesh):
    devices = mesh.shape["ctx"] * mesh.shape["head"]

    def body(queries, *rest):
        rows, width = queries.shape
        one_each = width == devices * HEAD_DIM and rows % (4 * BLOCK_TOK) == 0
        return (one_head_each if one_each else halo_exchange)(queries, *rest)

    tokens = P(("band", "ctx", "head"), None)
    return jax.shard_map(
        body,
        mesh=mesh,
        in_specs=(tokens,) * 4 + (P("band"), P("band", None)),
        out_specs=(tokens,) * 3,
        check_vma=False,
    )
```

```python
import math

import jax
import jax.numpy as jnp
from jax import lax
from jax.experimental import pallas as pl
from jax.experimental.pallas import tpu as pltpu
from jax.sharding import PartitionSpec as P

HEAD_DIM = 64
BLOCK_TOK = 64
NBR = 8
REACH = 1
PAIR = 2 * HEAD_DIM
LIST_ROWS = NBR * BLOCK_TOK
SCALE = HEAD_DIM ** -0.5
EXP2_SCALE = SCALE * math.log2(math.e)
SUBLANES = 8
CHUNK = 16
VMEM_LIMIT = 48 * 1024 * 1024
PACK_VMEM_LIMIT = 60 * 1024 * 1024
NT = (((1,), (1,)), ((), ()))
NN = (((1,), (0,)), ((), ()))
TN = (((0,), (0,)), ((), ()))


def from_behind(value, axis, steps):
    count = lax.axis_size(axis)
    pairs = [(source, (source + steps) % count) for source in range(count)]
    return lax.ppermute(value, axis, pairs)


def call_kernel(kernel, out_shape, in_memory, scratch_shapes=(), **cost):
    outs = jax.tree.map(lambda _: pl.BlockSpec(memory_space=pltpu.VMEM), out_shape)
    return pl.pallas_call(
        kernel,
        out_shape=out_shape,
        in_specs=[pl.BlockSpec(memory_space=space) for space in in_memory],
        out_specs=outs,
        scratch_shapes=list(scratch_shapes),
        compiler_params=pltpu.CompilerParams(vmem_limit_bytes=VMEM_LIMIT),
        cost_estimate=pl.CostEstimate(**cost) if cost else None,
    )


def columns_of(ref, head):
    return ref[:, head * HEAD_DIM : (head + 1) * HEAD_DIM]


def pack_kernel(query_ref, grad_ref, key_ref, value_ref, out_ref):
    for head in range(out_ref.shape[0]):
        out_ref[head, 0] = jnp.concatenate([columns_of(query_ref, head), columns_of(grad_ref, head)], axis=1)
        out_ref[head, 1] = jnp.concatenate([columns_of(key_ref, head), columns_of(value_ref, head)], axis=1)


def unpack_kernel(packed_ref, query_ref, key_ref, value_ref):
    rows = query_ref.shape[0]
    for pair in range(packed_ref.shape[0] // 2):
        lanes = slice(pair * PAIR, (pair + 1) * PAIR)
        even, odd = packed_ref[2 * pair], packed_ref[2 * pair + 1]
        key_ref[:, lanes] = jnp.concatenate([even[:rows, :HEAD_DIM], odd[:rows, :HEAD_DIM]], axis=1)
        value_ref[:, lanes] = jnp.concatenate([even[:rows, HEAD_DIM:], odd[:rows, HEAD_DIM:]], axis=1)
        for place in range(rows // (2 * BLOCK_TOK)):
            start = rows + place * BLOCK_TOK
            part = slice(start, start + BLOCK_TOK)
            first = slice(2 * place * BLOCK_TOK, (2 * place + 1) * BLOCK_TOK)
            second = slice((2 * place + 1) * BLOCK_TOK, (2 * place + 2) * BLOCK_TOK)
            query_ref[first, lanes] = jnp.concatenate([even[part, :HEAD_DIM], odd[part, :HEAD_DIM]], axis=1)
            query_ref[second, lanes] = jnp.concatenate([even[part, HEAD_DIM:], odd[part, HEAD_DIM:]], axis=1)


def diagonal_of(rows):
    low = lax.broadcasted_iota(jnp.int32, (BLOCK_TOK, PAIR), 1) < HEAD_DIM
    rows_a, rows_b = rows[:BLOCK_TOK], rows[BLOCK_TOK:]
    zero = jnp.zeros_like(rows_a)
    return jnp.concatenate(
        [
            jnp.concatenate([jnp.where(low, rows_a, zero), zero], axis=1),
            jnp.concatenate([zero, jnp.where(low, rows_b, zero)], axis=1),
            jnp.concatenate([jnp.where(low, zero, rows_a), zero], axis=1),
            jnp.concatenate([zero, jnp.where(low, zero, rows_b)], axis=1),
        ],
        axis=0,
    )


def swap_halves(rows):
    return jnp.concatenate([rows[:, HEAD_DIM:], rows[:, :HEAD_DIM]], axis=1)


def fold_rows(value, reduce):
    return reduce(value.reshape(-1, SUBLANES, PAIR), axis=0)


def accumulate_blocks(
    pairs, list_ref, place_ref, query_pair, key_value_rows, value_key_rows, write_query, acc_ref, buffers
):
    count = 2 * NBR

    def listed_of(pair):
        starts = [pl.multiple_of(list_ref[pair * count + n], BLOCK_TOK) for n in range(count)]
        blocks = [key_value_rows(start) for start in starts]
        return jnp.concatenate(
            [jnp.concatenate(blocks[:NBR], axis=0), jnp.concatenate(blocks[NBR:], axis=0)], axis=1
        )

    def listed_keys(pair):
        low = lax.broadcasted_iota(jnp.int32, (BLOCK_TOK, PAIR), 1) < HEAD_DIM
        starts = [pl.multiple_of(list_ref[pair * count + n], BLOCK_TOK) for n in range(count)]
        return jnp.concatenate(
            [
                jnp.where(low, key_value_rows(starts[n]), value_key_rows(starts[NBR + n]))
                for n in range(NBR)
            ],
            axis=0,
        )

    def scores_stage(pair, buffer):
        both_ref, _ = buffer
        both_ref[...] = lax.dot_general(
            listed_of(pair), diagonal_of(query_pair(pair)), NT, preferred_element_type=jnp.float32
        )

    def softmax_stage(buffer):
        both_ref, low_ref = buffer
        chunks = [slice(start, start + CHUNK) for start in range(0, LIST_ROWS, CHUNK)]
        top = None
        for rows in chunks:
            part = fold_rows(both_ref[rows, :PAIR], jnp.max)
            top = part if top is None else jnp.maximum(top, part)
        top = jnp.max(top, axis=0, keepdims=True) * EXP2_SCALE
        total = delta = None
        for rows in chunks:
            weights = jnp.exp2(both_ref[rows, :PAIR] * EXP2_SCALE - top)
            part, part_delta = fold_rows(weights, jnp.sum), fold_rows(weights * both_ref[rows, PAIR:], jnp.sum)
            both_ref[rows, :PAIR] = weights
            total = part if total is None else total + part
            delta = part_delta if delta is None else delta + part_delta
        inverse = 1.0 / jnp.sum(total, axis=0, keepdims=True)
        row_delta = jnp.sum(delta, axis=0, keepdims=True) * inverse
        for rows in chunks:
            probability = both_ref[rows, :PAIR] * inverse
            grad_score = probability * (both_ref[rows, PAIR:] - row_delta)
            low_ref[rows, :PAIR] = grad_score.astype(jnp.bfloat16)
            low_ref[rows, PAIR:] = probability.astype(jnp.bfloat16)

    def gradients_stage(pair, buffer):
        _, low_ref = buffer
        grad_listed = lax.dot_general(
            low_ref[...], diagonal_of(query_pair(pair)), NN, preferred_element_type=jnp.float32
        )
        for n in range(NBR):
            for side in range(2):
                start = pl.multiple_of(place_ref[pair * count + side * NBR + n], BLOCK_TOK)
                acc_ref[pl.ds(start, BLOCK_TOK)] += grad_listed[
                    n * BLOCK_TOK : (n + 1) * BLOCK_TOK, side * PAIR : (side + 1) * PAIR
                ]
        grad_query = lax.dot_general(
            low_ref[:, :PAIR], listed_keys(pair), TN, preferred_element_type=jnp.float32
        )
        low = lax.broadcasted_iota(jnp.int32, (BLOCK_TOK, PAIR), 1) < HEAD_DIM
        write_query(pair, jnp.where(low, grad_query[:BLOCK_TOK], grad_query[BLOCK_TOK:]) * SCALE)

    even, odd = buffers[:2], buffers[2:]
    acc_ref[...] = jnp.zeros_like(acc_ref)
    scores_stage(0, even)
    softmax_stage(even)
    scores_stage(1, odd)

    def step(index, carry):
        pair = 2 * index
        gradients_stage(pair, even)
        softmax_stage(odd)
        scores_stage(pair + 2, even)
        gradients_stage(pair + 1, odd)
        softmax_stage(even)
        scores_stage(pair + 3, odd)
        return carry

    lax.fori_loop(0, pairs // 2 - 1, step, 0)
    gradients_stage(pairs - 2, even)
    softmax_stage(odd)
    gradients_stage(pairs - 1, odd)


def key_scale():
    low = lax.broadcasted_iota(jnp.int32, (1, PAIR), 1) < HEAD_DIM
    return jnp.where(low, jnp.float32(SCALE), jnp.float32(1.0))


def head_kernel(list_ref, place_ref, packed_ref, out_ref, acc_ref, swap_ref, *buffers):
    sources, out_rows, _ = out_ref.shape
    rows = 2 * out_rows // 3
    pairs_each = rows // (2 * BLOCK_TOK)

    def query_pair(pair):
        start = pair // pairs_each * (2 * rows) + pair % pairs_each * (2 * BLOCK_TOK)
        return packed_ref[pl.ds(pl.multiple_of(start, 2 * BLOCK_TOK), 2 * BLOCK_TOK)]

    def write_query(pair, value):
        start = rows + pl.multiple_of(pair % pairs_each * BLOCK_TOK, BLOCK_TOK)
        out_ref[pair // pairs_each, pl.ds(start, BLOCK_TOK)] = value.astype(jnp.bfloat16)

    for source in range(sources):
        part = slice((2 * source + 1) * rows, (2 * source + 2) * rows)
        swap_ref[part] = swap_halves(packed_ref[part])
    accumulate_blocks(
        sources * pairs_each,
        list_ref,
        place_ref,
        query_pair,
        lambda start: packed_ref[pl.ds(start, BLOCK_TOK)],
        lambda start: swap_ref[pl.ds(start, BLOCK_TOK)],
        write_query,
        acc_ref,
        buffers,
    )

    def write(source, carry):
        start = pl.multiple_of(source * rows, rows)
        out_ref[source, :rows] = (acc_ref[pl.ds(start, rows)] * key_scale()).astype(jnp.bfloat16)
        return carry

    lax.fori_loop(0, sources, write, 0)


def work_buffers():
    return [
        pltpu.VMEM((LIST_ROWS, 2 * PAIR), jnp.float32),
        pltpu.VMEM((LIST_ROWS, 2 * PAIR), jnp.bfloat16),
    ] * 2


def listed_slots(block_slot, neighbours):
    slot_ids = jnp.arange(block_slot.shape[0], dtype=jnp.int32)
    matches = (block_slot[None, :] == slot_ids[:, None]).astype(jnp.int32)
    sphere_of = jnp.sum(matches * slot_ids[None, :], axis=1)
    return block_slot[neighbours[sphere_of]]


def one_head_each(queries, key_states, value_states, grad_output, block_slot, neighbours):
    axes = ("ctx", "head")
    rows, width = queries.shape
    heads = width // HEAD_DIM
    tokens = heads * rows
    in_vmem, in_smem = pltpu.VMEM, pltpu.SMEM
    packed = pl.pallas_call(
        pack_kernel,
        grid=(2,),
        in_specs=[pl.BlockSpec((rows // 2, width), lambda i: (i, 0))] * 4,
        out_specs=pl.BlockSpec((heads, 2, rows // 2, PAIR), lambda i: (0, 0, i, 0)),
        out_shape=jax.ShapeDtypeStruct((heads, 2, rows, PAIR), jnp.bfloat16),
        compiler_params=pltpu.CompilerParams(vmem_limit_bytes=PACK_VMEM_LIMIT),
    )(queries, grad_output, key_states, value_states)
    packed = lax.all_to_all(packed, axes, split_axis=0, concat_axis=0, tiled=True)
    place = listed_slots(block_slot, neighbours).reshape(-1) * BLOCK_TOK
    start = place // rows * (2 * rows) + rows + place % rows
    grads = call_kernel(
        head_kernel,
        jax.ShapeDtypeStruct((heads, 3 * rows // 2, PAIR), jnp.bfloat16),
        [in_smem, in_smem, in_vmem],
        [pltpu.VMEM((tokens, PAIR), jnp.float32), pltpu.VMEM((2 * tokens, PAIR), jnp.bfloat16)]
        + work_buffers(),
        flops=10 * tokens * LIST_ROWS * HEAD_DIM,
        bytes_accessed=7 * tokens * PAIR,
        transcendentals=tokens * LIST_ROWS,
    )(start, place, packed.reshape(2 * tokens, PAIR))
    grads = lax.all_to_all(grads, axes, split_axis=0, concat_axis=0, tiled=True)
    return call_kernel(
        unpack_kernel,
        (jax.ShapeDtypeStruct((rows, width), jnp.bfloat16),) * 3,
        [in_vmem],
    )(grads)


def halo_kernel(list_ref, query_ref, key_value_ref, grad_query_out, acc_out, swap_ref, *buffers):
    for head in range(query_ref.shape[0]):
        swap_ref[...] = swap_halves(key_value_ref[head])

        def write_query(pair, value):
            grad_query_out[head, pl.ds(pl.multiple_of(pair * BLOCK_TOK, BLOCK_TOK), BLOCK_TOK)] = value

        accumulate_blocks(
            query_ref.shape[1] // (2 * BLOCK_TOK),
            list_ref,
            list_ref,
            lambda pair: query_ref[head, pl.ds(pl.multiple_of(pair * 2 * BLOCK_TOK, 2 * BLOCK_TOK), 2 * BLOCK_TOK)],
            lambda start: key_value_ref[head, pl.ds(start, BLOCK_TOK)],
            lambda start: swap_ref[pl.ds(start, BLOCK_TOK)],
            write_query,
            acc_out.at[head],
            buffers,
        )
        acc_out[head] = acc_out[head] * key_scale()


def halo_exchange(queries, key_states, value_states, grad_output, block_slot, neighbours):
    def to_heads(value):
        return lax.all_to_all(value, "head", split_axis=1, concat_axis=0, tiled=True)

    def paired(left, right):
        parts = [to_heads(x).reshape(-1, heads, 1, HEAD_DIM) for x in (left, right)]
        both = jnp.concatenate(parts, axis=2)
        return jnp.moveaxis(both, 1, 0).reshape(heads, -1, PAIR)

    heads = queries.shape[1] // HEAD_DIM // lax.axis_size("head")
    query_side = paired(queries, grad_output)
    key_side = paired(key_states, value_states)
    rows = query_side.shape[1]
    blocks = rows // BLOCK_TOK
    ctx_size = lax.axis_size("ctx")
    ctx_here = lax.axis_index("ctx")
    listed = lax.dynamic_slice_in_dim(listed_slots(block_slot, neighbours), ctx_here * blocks, blocks, 0)
    gap = (listed // blocks - ctx_here + ctx_size + REACH) % ctx_size - REACH
    lookup = (gap + REACH) * blocks + listed % blocks
    offsets = range(-REACH, REACH + 1)
    span = jnp.concatenate(
        [key_side if o == 0 else from_behind(key_side, "ctx", -o) for o in offsets], axis=1
    )
    grad_query, partial = call_kernel(
        halo_kernel,
        (
            jax.ShapeDtypeStruct((heads, rows // 2, PAIR), jnp.float32),
            jax.ShapeDtypeStruct(span.shape, jnp.float32),
        ),
        [pltpu.SMEM, pltpu.VMEM, pltpu.VMEM],
        [pltpu.VMEM(span.shape[1:], jnp.bfloat16)] + work_buffers(),
    )(lookup.reshape(-1) * BLOCK_TOK, query_side, span)
    returned = partial.reshape(heads, 2 * REACH + 1, rows, PAIR)
    summed = returned[:, REACH]
    for offset in offsets:
        if offset != 0:
            summed = summed + from_behind(returned[:, offset + REACH], "ctx", offset)

    def to_tokens(value):
        value = jnp.moveaxis(value.astype(jnp.bfloat16), 0, 1).reshape(rows, heads * HEAD_DIM)
        return lax.all_to_all(value, "head", split_axis=0, concat_axis=1, tiled=True)

    grad_query = grad_query.reshape(heads, blocks // 2, BLOCK_TOK, 2, HEAD_DIM)
    return (
        to_tokens(jnp.swapaxes(grad_query, 2, 3).reshape(heads, rows, HEAD_DIM)),
        to_tokens(summed[..., :HEAD_DIM]),
        to_tokens(summed[..., HEAD_DIM:]),
    )


def solution(mesh):
    devices = mesh.shape["ctx"] * mesh.shape["head"]

    def body(queries, *rest):
        rows, width = queries.shape
        one_each = width == devices * HEAD_DIM and rows % (4 * BLOCK_TOK) == 0
        return (one_head_each if one_each else halo_exchange)(queries, *rest)

    tokens = P(("band", "ctx", "head"), None)
    return jax.shard_map(
        body,
        mesh=mesh,
        in_specs=(tokens,) * 4 + (P("band"), P("band", None)),
        out_specs=(tokens,) * 3,
        check_vma=False,
    )
```

```python
import math

import jax
import jax.numpy as jnp
from jax import lax
from jax.experimental import pallas as pl
from jax.experimental.pallas import tpu as pltpu
from jax.sharding import PartitionSpec as P

HEAD_DIM = 64
BLOCK_TOK = 64
NBR = 8
REACH = 1
PAIR = 2 * HEAD_DIM
LIST_ROWS = NBR * BLOCK_TOK
SCALE = HEAD_DIM ** -0.5
EXP2_SCALE = SCALE * math.log2(math.e)
SUBLANES = 8
CHUNK = 32
VMEM_LIMIT = 48 * 1024 * 1024
PACK_VMEM_LIMIT = 60 * 1024 * 1024
NT = (((1,), (1,)), ((), ()))
NN = (((1,), (0,)), ((), ()))
TN = (((0,), (0,)), ((), ()))


def from_behind(value, axis, steps):
    count = lax.axis_size(axis)
    pairs = [(source, (source + steps) % count) for source in range(count)]
    return lax.ppermute(value, axis, pairs)


def call_kernel(kernel, out_shape, in_memory, scratch_shapes=(), **cost):
    outs = jax.tree.map(lambda _: pl.BlockSpec(memory_space=pltpu.VMEM), out_shape)
    return pl.pallas_call(
        kernel,
        out_shape=out_shape,
        in_specs=[pl.BlockSpec(memory_space=space) for space in in_memory],
        out_specs=outs,
        scratch_shapes=list(scratch_shapes),
        compiler_params=pltpu.CompilerParams(vmem_limit_bytes=VMEM_LIMIT),
        cost_estimate=pl.CostEstimate(**cost) if cost else None,
    )


def columns_of(ref, head):
    return ref[:, head * HEAD_DIM : (head + 1) * HEAD_DIM]


def pack_kernel(query_ref, grad_ref, key_ref, value_ref, out_ref):
    for head in range(out_ref.shape[0]):
        out_ref[head, 0] = jnp.concatenate([columns_of(query_ref, head), columns_of(grad_ref, head)], axis=1)
        out_ref[head, 1] = jnp.concatenate([columns_of(key_ref, head), columns_of(value_ref, head)], axis=1)


def unpack_kernel(packed_ref, query_ref, key_ref, value_ref, held, sems):
    rows, width = query_ref.shape
    heads = packed_ref.shape[0]

    def halves(pair, part, lanes):
        return jnp.concatenate([packed_ref[2 * pair, part, lanes], packed_ref[2 * pair + 1, part, lanes]], axis=1)

    def columns(pair):
        return slice(pair * PAIR, (pair + 1) * PAIR)

    copies = []
    first, second = slice(0, HEAD_DIM), slice(HEAD_DIM, PAIR)
    for n, (out_ref, lanes) in enumerate(((key_ref, first), (value_ref, second))):
        for pair in range(heads // 2):
            held[n, :, columns(pair)] = halves(pair, slice(0, rows), lanes)
        copies.append(pltpu.make_async_copy(held.at[n], out_ref, sems.at[n]))
        copies[-1].start()
    for place in range(rows // BLOCK_TOK):
        start = rows + place // 2 * BLOCK_TOK
        lanes = second if place % 2 else first
        for pair in range(heads // 2):
            held[2, place * BLOCK_TOK : (place + 1) * BLOCK_TOK, columns(pair)] = halves(
                pair, slice(start, start + BLOCK_TOK), lanes
            )
    copies.append(pltpu.make_async_copy(held.at[2], query_ref, sems.at[2]))
    copies[-1].start()
    for copy in copies:
        copy.wait()


def diagonal_of(rows):
    low = lax.broadcasted_iota(jnp.int32, (BLOCK_TOK, PAIR), 1) < HEAD_DIM
    rows_a, rows_b = rows[:BLOCK_TOK], rows[BLOCK_TOK:]
    zero = jnp.zeros_like(rows_a)
    return jnp.concatenate(
        [
            jnp.concatenate([jnp.where(low, rows_a, zero), zero], axis=1),
            jnp.concatenate([zero, jnp.where(low, rows_b, zero)], axis=1),
            jnp.concatenate([jnp.where(low, zero, rows_a), zero], axis=1),
            jnp.concatenate([zero, jnp.where(low, zero, rows_b)], axis=1),
        ],
        axis=0,
    )


def swap_halves(rows):
    return jnp.concatenate([rows[:, HEAD_DIM:], rows[:, :HEAD_DIM]], axis=1)


def fold_rows(value, reduce):
    return reduce(value.reshape(-1, SUBLANES, PAIR), axis=0)


def accumulate_blocks(
    pairs, list_ref, place_ref, query_pair, key_value_rows, value_key_rows, write_query, acc_ref, buffers
):
    count = 2 * NBR

    def listed_of(pair):
        starts = [pl.multiple_of(list_ref[pair * count + n], BLOCK_TOK) for n in range(count)]
        blocks = [key_value_rows(start) for start in starts]
        return jnp.concatenate(
            [jnp.concatenate(blocks[:NBR], axis=0), jnp.concatenate(blocks[NBR:], axis=0)], axis=1
        )

    def listed_keys(pair):
        low = lax.broadcasted_iota(jnp.int32, (BLOCK_TOK, PAIR), 1) < HEAD_DIM
        starts = [pl.multiple_of(list_ref[pair * count + n], BLOCK_TOK) for n in range(count)]
        return jnp.concatenate(
            [
                jnp.where(low, key_value_rows(starts[n]), value_key_rows(starts[NBR + n]))
                for n in range(NBR)
            ],
            axis=0,
        )

    def scores_stage(pair, buffer):
        both_ref, stat_ref = buffer
        both = lax.dot_general(
            listed_of(pair), diagonal_of(query_pair(pair)), NT, preferred_element_type=jnp.float32
        )
        both_ref[...] = both
        stat_ref[...] = fold_rows(both[:, :PAIR], jnp.max)

    def softmax_stage(buffer):
        both_ref, stat_ref = buffer
        top = jnp.max(stat_ref[...], axis=0, keepdims=True) * EXP2_SCALE
        total = delta = None
        for start in range(0, LIST_ROWS, CHUNK):
            rows = slice(start, start + CHUNK)
            weights = jnp.exp2(both_ref[rows, :PAIR] * EXP2_SCALE - top)
            part, part_delta = fold_rows(weights, jnp.sum), fold_rows(weights * both_ref[rows, PAIR:], jnp.sum)
            both_ref[rows, :PAIR] = weights
            total = part if total is None else total + part
            delta = part_delta if delta is None else delta + part_delta
        inverse = 1.0 / jnp.sum(total, axis=0, keepdims=True)
        stat_ref[0:1] = inverse
        stat_ref[1:2] = jnp.sum(delta, axis=0, keepdims=True) * inverse

    def gradients_stage(pair, buffer):
        both_ref, stat_ref = buffer
        inverse, row_delta = stat_ref[0:1], stat_ref[1:2]
        probability = both_ref[:, :PAIR] * inverse
        score_low = (probability * (both_ref[:, PAIR:] - row_delta)).astype(jnp.bfloat16)
        grad_listed = lax.dot_general(
            jnp.concatenate([score_low, probability.astype(jnp.bfloat16)], axis=1),
            diagonal_of(query_pair(pair)),
            NN,
            preferred_element_type=jnp.float32,
        )
        for n in range(NBR):
            for side in range(2):
                start = pl.multiple_of(place_ref[pair * count + side * NBR + n], BLOCK_TOK)
                acc_ref[pl.ds(start, BLOCK_TOK)] += grad_listed[
                    n * BLOCK_TOK : (n + 1) * BLOCK_TOK, side * PAIR : (side + 1) * PAIR
                ]
        grad_query = lax.dot_general(score_low, listed_keys(pair), TN, preferred_element_type=jnp.float32)
        low = lax.broadcasted_iota(jnp.int32, (BLOCK_TOK, PAIR), 1) < HEAD_DIM
        write_query(pair, jnp.where(low, grad_query[:BLOCK_TOK], grad_query[BLOCK_TOK:]) * SCALE)

    even, odd = buffers[:2], buffers[2:]
    acc_ref[...] = jnp.zeros_like(acc_ref)
    scores_stage(0, even)
    softmax_stage(even)
    scores_stage(1, odd)

    def step(index, carry):
        pair = 2 * index
        gradients_stage(pair, even)
        softmax_stage(odd)
        scores_stage(pair + 2, even)
        gradients_stage(pair + 1, odd)
        softmax_stage(even)
        scores_stage(pair + 3, odd)
        return carry

    lax.fori_loop(0, pairs // 2 - 1, step, 0)
    gradients_stage(pairs - 2, even)
    softmax_stage(odd)
    gradients_stage(pairs - 1, odd)


def key_scale():
    low = lax.broadcasted_iota(jnp.int32, (1, PAIR), 1) < HEAD_DIM
    return jnp.where(low, jnp.float32(SCALE), jnp.float32(1.0))


def head_kernel(list_ref, place_ref, packed_ref, out_ref, acc_ref, swap_ref, *buffers):
    sources, out_rows, _ = out_ref.shape
    rows = 2 * out_rows // 3
    pairs_each = rows // (2 * BLOCK_TOK)

    def query_pair(pair):
        start = pair // pairs_each * (2 * rows) + pair % pairs_each * (2 * BLOCK_TOK)
        return packed_ref[pl.ds(pl.multiple_of(start, 2 * BLOCK_TOK), 2 * BLOCK_TOK)]

    def write_query(pair, value):
        start = rows + pl.multiple_of(pair % pairs_each * BLOCK_TOK, BLOCK_TOK)
        out_ref[pair // pairs_each, pl.ds(start, BLOCK_TOK)] = value.astype(jnp.bfloat16)

    for source in range(sources):
        part = slice((2 * source + 1) * rows, (2 * source + 2) * rows)
        swap_ref[part] = swap_halves(packed_ref[part])
    accumulate_blocks(
        sources * pairs_each,
        list_ref,
        place_ref,
        query_pair,
        lambda start: packed_ref[pl.ds(start, BLOCK_TOK)],
        lambda start: swap_ref[pl.ds(start, BLOCK_TOK)],
        write_query,
        acc_ref,
        buffers,
    )

    def write(source, carry):
        start = pl.multiple_of(source * rows, rows)
        out_ref[source, :rows] = (acc_ref[pl.ds(start, rows)] * key_scale()).astype(jnp.bfloat16)
        return carry

    lax.fori_loop(0, sources, write, 0)


def work_buffers():
    return [
        pltpu.VMEM((LIST_ROWS, 2 * PAIR), jnp.float32),
        pltpu.VMEM((SUBLANES, PAIR), jnp.float32),
    ] * 2


def listed_slots(block_slot, neighbours):
    slot_ids = jnp.arange(block_slot.shape[0], dtype=jnp.int32)
    matches = (block_slot[None, :] == slot_ids[:, None]).astype(jnp.int32)
    sphere_of = jnp.sum(matches * slot_ids[None, :], axis=1)
    return block_slot[neighbours[sphere_of]]


def one_head_each(queries, key_states, value_states, grad_output, block_slot, neighbours):
    axes = ("ctx", "head")
    rows, width = queries.shape
    heads = width // HEAD_DIM
    tokens = heads * rows
    in_vmem, in_smem = pltpu.VMEM, pltpu.SMEM
    packed = pl.pallas_call(
        pack_kernel,
        grid=(2,),
        in_specs=[pl.BlockSpec((rows // 2, width), lambda i: (i, 0))] * 4,
        out_specs=pl.BlockSpec((heads, 2, rows // 2, PAIR), lambda i: (0, 0, i, 0)),
        out_shape=jax.ShapeDtypeStruct((heads, 2, rows, PAIR), jnp.bfloat16),
        compiler_params=pltpu.CompilerParams(vmem_limit_bytes=PACK_VMEM_LIMIT),
    )(queries, grad_output, key_states, value_states)
    packed = lax.all_to_all(packed, axes, split_axis=0, concat_axis=0, tiled=True)
    place = listed_slots(block_slot, neighbours).reshape(-1) * BLOCK_TOK
    start = place // rows * (2 * rows) + rows + place % rows
    grads = call_kernel(
        head_kernel,
        jax.ShapeDtypeStruct((heads, 3 * rows // 2, PAIR), jnp.bfloat16),
        [in_smem, in_smem, in_vmem],
        [pltpu.VMEM((tokens, PAIR), jnp.float32), pltpu.VMEM((2 * tokens, PAIR), jnp.bfloat16)]
        + work_buffers(),
        flops=10 * tokens * LIST_ROWS * HEAD_DIM,
        bytes_accessed=7 * tokens * PAIR,
        transcendentals=tokens * LIST_ROWS,
    )(start, place, packed.reshape(2 * tokens, PAIR))
    grads = lax.all_to_all(grads, axes, split_axis=0, concat_axis=0, tiled=True)
    return pl.pallas_call(
        unpack_kernel,
        out_shape=(jax.ShapeDtypeStruct((rows, width), jnp.bfloat16),) * 3,
        in_specs=[pl.BlockSpec(memory_space=in_vmem)],
        out_specs=(pl.BlockSpec(memory_space=pl.ANY),) * 3,
        scratch_shapes=[pltpu.VMEM((3, rows, width), jnp.bfloat16), pltpu.SemaphoreType.DMA((3,))],
        compiler_params=pltpu.CompilerParams(vmem_limit_bytes=VMEM_LIMIT),
    )(grads)


def halo_kernel(list_ref, query_ref, key_value_ref, grad_query_out, acc_out, swap_ref, *buffers):
    for head in range(query_ref.shape[0]):
        swap_ref[...] = swap_halves(key_value_ref[head])

        def write_query(pair, value):
            grad_query_out[head, pl.ds(pl.multiple_of(pair * BLOCK_TOK, BLOCK_TOK), BLOCK_TOK)] = value

        accumulate_blocks(
            query_ref.shape[1] // (2 * BLOCK_TOK),
            list_ref,
            list_ref,
            lambda pair: query_ref[head, pl.ds(pl.multiple_of(pair * 2 * BLOCK_TOK, 2 * BLOCK_TOK), 2 * BLOCK_TOK)],
            lambda start: key_value_ref[head, pl.ds(start, BLOCK_TOK)],
            lambda start: swap_ref[pl.ds(start, BLOCK_TOK)],
            write_query,
            acc_out.at[head],
            buffers,
        )
        acc_out[head] = acc_out[head] * key_scale()


def halo_exchange(queries, key_states, value_states, grad_output, block_slot, neighbours):
    def to_heads(value):
        return lax.all_to_all(value, "head", split_axis=1, concat_axis=0, tiled=True)

    def paired(left, right):
        parts = [to_heads(x).reshape(-1, heads, 1, HEAD_DIM) for x in (left, right)]
        both = jnp.concatenate(parts, axis=2)
        return jnp.moveaxis(both, 1, 0).reshape(heads, -1, PAIR)

    heads = queries.shape[1] // HEAD_DIM // lax.axis_size("head")
    query_side = paired(queries, grad_output)
    key_side = paired(key_states, value_states)
    rows = query_side.shape[1]
    blocks = rows // BLOCK_TOK
    ctx_size = lax.axis_size("ctx")
    ctx_here = lax.axis_index("ctx")
    listed = lax.dynamic_slice_in_dim(listed_slots(block_slot, neighbours), ctx_here * blocks, blocks, 0)
    gap = (listed // blocks - ctx_here + ctx_size + REACH) % ctx_size - REACH
    lookup = (gap + REACH) * blocks + listed % blocks
    offsets = range(-REACH, REACH + 1)
    span = jnp.concatenate(
        [key_side if o == 0 else from_behind(key_side, "ctx", -o) for o in offsets], axis=1
    )
    grad_query, partial = call_kernel(
        halo_kernel,
        (
            jax.ShapeDtypeStruct((heads, rows // 2, PAIR), jnp.float32),
            jax.ShapeDtypeStruct(span.shape, jnp.float32),
        ),
        [pltpu.SMEM, pltpu.VMEM, pltpu.VMEM],
        [pltpu.VMEM(span.shape[1:], jnp.bfloat16)] + work_buffers(),
    )(lookup.reshape(-1) * BLOCK_TOK, query_side, span)
    returned = partial.reshape(heads, 2 * REACH + 1, rows, PAIR)
    summed = returned[:, REACH]
    for offset in offsets:
        if offset != 0:
            summed = summed + from_behind(returned[:, offset + REACH], "ctx", offset)

    def to_tokens(value):
        value = jnp.moveaxis(value.astype(jnp.bfloat16), 0, 1).reshape(rows, heads * HEAD_DIM)
        return lax.all_to_all(value, "head", split_axis=0, concat_axis=1, tiled=True)

    grad_query = grad_query.reshape(heads, blocks // 2, BLOCK_TOK, 2, HEAD_DIM)
    return (
        to_tokens(jnp.swapaxes(grad_query, 2, 3).reshape(heads, rows, HEAD_DIM)),
        to_tokens(summed[..., :HEAD_DIM]),
        to_tokens(summed[..., HEAD_DIM:]),
    )


def solution(mesh):
    devices = mesh.shape["ctx"] * mesh.shape["head"]

    def body(queries, *rest):
        rows, width = queries.shape
        one_each = width == devices * HEAD_DIM and rows % (4 * BLOCK_TOK) == 0
        return (one_head_each if one_each else halo_exchange)(queries, *rest)

    tokens = P(("band", "ctx", "head"), None)
    return jax.shard_map(
        body,
        mesh=mesh,
        in_specs=(tokens,) * 4 + (P("band"), P("band", None)),
        out_specs=(tokens,) * 3,
        check_vma=False,
    )
```

```python
import math

import jax
import jax.numpy as jnp
from jax import lax
from jax.experimental import pallas as pl
from jax.experimental.pallas import tpu as pltpu
from jax.sharding import PartitionSpec as P

HEAD_DIM = 64
BLOCK_TOK = 64
NBR = 8
REACH = 1
PAIR = 2 * HEAD_DIM
LIST_ROWS = NBR * BLOCK_TOK
SCALE = HEAD_DIM ** -0.5
EXP2_SCALE = SCALE * math.log2(math.e)
SUBLANES = 8
CHUNK = 32
VMEM_LIMIT = 48 * 1024 * 1024
PACK_VMEM_LIMIT = 60 * 1024 * 1024
NT = (((1,), (1,)), ((), ()))
NN = (((1,), (0,)), ((), ()))
TN = (((0,), (0,)), ((), ()))


def from_behind(value, axis, steps):
    count = lax.axis_size(axis)
    pairs = [(source, (source + steps) % count) for source in range(count)]
    return lax.ppermute(value, axis, pairs)


def call_kernel(kernel, out_shape, in_memory, scratch_shapes=(), **cost):
    outs = jax.tree.map(lambda _: pl.BlockSpec(memory_space=pltpu.VMEM), out_shape)
    return pl.pallas_call(
        kernel,
        out_shape=out_shape,
        in_specs=[pl.BlockSpec(memory_space=space) for space in in_memory],
        out_specs=outs,
        scratch_shapes=list(scratch_shapes),
        compiler_params=pltpu.CompilerParams(vmem_limit_bytes=VMEM_LIMIT),
        cost_estimate=pl.CostEstimate(**cost) if cost else None,
    )


def columns_of(ref, head):
    return ref[:, head * HEAD_DIM : (head + 1) * HEAD_DIM]


def pack_kernel(query_ref, grad_ref, key_ref, value_ref, out_ref, held, ready, in_sems, out_sems):
    heads = out_ref.shape[0]
    groups = out_sems.shape[1]
    some = heads // groups
    arrays = (query_ref, grad_ref, key_ref, value_ref)
    loads = [pltpu.make_async_copy(array, held.at[n], in_sems.at[n]) for n, array in enumerate(arrays)]
    for load in loads:
        load.start()
    stores = []
    for kind in range(2):
        left, right = 2 * kind, 2 * kind + 1
        loads[left].wait()
        loads[right].wait()
        for group in range(groups):
            for head in range(group * some, (group + 1) * some):
                ready[head, kind] = jnp.concatenate(
                    [columns_of(held.at[left], head), columns_of(held.at[right], head)], axis=1
                )
            part = pl.ds(group * some, some)
            stores.append(
                pltpu.make_async_copy(ready.at[part, kind], out_ref.at[part, kind], out_sems.at[kind, group])
            )
            stores[-1].start()
    for store in stores:
        store.wait()


def unpack_kernel(packed_ref, query_ref, key_ref, value_ref, held, sems):
    rows, width = query_ref.shape
    heads = packed_ref.shape[0]

    def halves(pair, part, lanes):
        return jnp.concatenate([packed_ref[2 * pair, part, lanes], packed_ref[2 * pair + 1, part, lanes]], axis=1)

    def columns(pair):
        return slice(pair * PAIR, (pair + 1) * PAIR)

    copies = []
    first, second = slice(0, HEAD_DIM), slice(HEAD_DIM, PAIR)
    for n, (out_ref, lanes) in enumerate(((key_ref, first), (value_ref, second))):
        for pair in range(heads // 2):
            held[n, :, columns(pair)] = halves(pair, slice(0, rows), lanes)
        copies.append(pltpu.make_async_copy(held.at[n], out_ref, sems.at[n]))
        copies[-1].start()
    for place in range(rows // BLOCK_TOK):
        start = rows + place // 2 * BLOCK_TOK
        lanes = second if place % 2 else first
        for pair in range(heads // 2):
            held[2, place * BLOCK_TOK : (place + 1) * BLOCK_TOK, columns(pair)] = halves(
                pair, slice(start, start + BLOCK_TOK), lanes
            )
    copies.append(pltpu.make_async_copy(held.at[2], query_ref, sems.at[2]))
    copies[-1].start()
    for copy in copies:
        copy.wait()


def diagonal_of(rows):
    low = lax.broadcasted_iota(jnp.int32, (BLOCK_TOK, PAIR), 1) < HEAD_DIM
    rows_a, rows_b = rows[:BLOCK_TOK], rows[BLOCK_TOK:]
    zero = jnp.zeros_like(rows_a)
    return jnp.concatenate(
        [
            jnp.concatenate([jnp.where(low, rows_a, zero), zero], axis=1),
            jnp.concatenate([zero, jnp.where(low, rows_b, zero)], axis=1),
            jnp.concatenate([jnp.where(low, zero, rows_a), zero], axis=1),
            jnp.concatenate([zero, jnp.where(low, zero, rows_b)], axis=1),
        ],
        axis=0,
    )


def swap_halves(rows):
    return jnp.concatenate([rows[:, HEAD_DIM:], rows[:, :HEAD_DIM]], axis=1)


def fold_rows(value, reduce):
    return reduce(value.reshape(-1, SUBLANES, PAIR), axis=0)


def accumulate_blocks(
    pairs, list_ref, place_ref, query_pair, key_value_rows, value_key_rows, write_query, acc_ref, buffers
):
    count = 2 * NBR

    def listed_of(pair):
        starts = [pl.multiple_of(list_ref[pair * count + n], BLOCK_TOK) for n in range(count)]
        blocks = [key_value_rows(start) for start in starts]
        return jnp.concatenate(
            [jnp.concatenate(blocks[:NBR], axis=0), jnp.concatenate(blocks[NBR:], axis=0)], axis=1
        )

    def listed_keys(pair):
        low = lax.broadcasted_iota(jnp.int32, (BLOCK_TOK, PAIR), 1) < HEAD_DIM
        starts = [pl.multiple_of(list_ref[pair * count + n], BLOCK_TOK) for n in range(count)]
        return jnp.concatenate(
            [
                jnp.where(low, key_value_rows(starts[n]), value_key_rows(starts[NBR + n]))
                for n in range(NBR)
            ],
            axis=0,
        )

    def scores_stage(pair, buffer):
        both_ref, stat_ref = buffer
        both = lax.dot_general(
            listed_of(pair), diagonal_of(query_pair(pair)), NT, preferred_element_type=jnp.float32
        )
        both_ref[...] = both
        stat_ref[...] = fold_rows(both[:, :PAIR], jnp.max)

    def softmax_stage(buffer):
        both_ref, stat_ref = buffer
        top = jnp.max(stat_ref[...], axis=0, keepdims=True) * EXP2_SCALE
        total = delta = None
        for start in range(0, LIST_ROWS, CHUNK):
            rows = slice(start, start + CHUNK)
            weights = jnp.exp2(both_ref[rows, :PAIR] * EXP2_SCALE - top)
            part, part_delta = fold_rows(weights, jnp.sum), fold_rows(weights * both_ref[rows, PAIR:], jnp.sum)
            both_ref[rows, :PAIR] = weights
            total = part if total is None else total + part
            delta = part_delta if delta is None else delta + part_delta
        inverse = 1.0 / jnp.sum(total, axis=0, keepdims=True)
        stat_ref[0:1] = inverse
        stat_ref[1:2] = jnp.sum(delta, axis=0, keepdims=True) * inverse

    def gradients_stage(pair, buffer):
        both_ref, stat_ref = buffer
        inverse, row_delta = stat_ref[0:1], stat_ref[1:2]
        probability = both_ref[:, :PAIR] * inverse
        score_low = (probability * (both_ref[:, PAIR:] - row_delta)).astype(jnp.bfloat16)
        grad_listed = lax.dot_general(
            jnp.concatenate([score_low, probability.astype(jnp.bfloat16)], axis=1),
            diagonal_of(query_pair(pair)),
            NN,
            preferred_element_type=jnp.float32,
        )
        for n in range(NBR):
            for side in range(2):
                start = pl.multiple_of(place_ref[pair * count + side * NBR + n], BLOCK_TOK)
                acc_ref[pl.ds(start, BLOCK_TOK)] += grad_listed[
                    n * BLOCK_TOK : (n + 1) * BLOCK_TOK, side * PAIR : (side + 1) * PAIR
                ]
        grad_query = lax.dot_general(score_low, listed_keys(pair), TN, preferred_element_type=jnp.float32)
        low = lax.broadcasted_iota(jnp.int32, (BLOCK_TOK, PAIR), 1) < HEAD_DIM
        write_query(pair, jnp.where(low, grad_query[:BLOCK_TOK], grad_query[BLOCK_TOK:]) * SCALE)

    even, odd = buffers[:2], buffers[2:]
    acc_ref[...] = jnp.zeros_like(acc_ref)
    scores_stage(0, even)
    softmax_stage(even)
    scores_stage(1, odd)

    def step(index, carry):
        pair = 2 * index
        gradients_stage(pair, even)
        softmax_stage(odd)
        scores_stage(pair + 2, even)
        gradients_stage(pair + 1, odd)
        softmax_stage(even)
        scores_stage(pair + 3, odd)
        return carry

    lax.fori_loop(0, pairs // 2 - 1, step, 0)
    gradients_stage(pairs - 2, even)
    softmax_stage(odd)
    gradients_stage(pairs - 1, odd)


def key_scale():
    low = lax.broadcasted_iota(jnp.int32, (1, PAIR), 1) < HEAD_DIM
    return jnp.where(low, jnp.float32(SCALE), jnp.float32(1.0))


def head_kernel(list_ref, place_ref, packed_ref, out_ref, acc_ref, swap_ref, *buffers):
    sources, out_rows, _ = out_ref.shape
    rows = 2 * out_rows // 3
    pairs_each = rows // (2 * BLOCK_TOK)

    def query_pair(pair):
        start = pair // pairs_each * (2 * rows) + pair % pairs_each * (2 * BLOCK_TOK)
        return packed_ref[pl.ds(pl.multiple_of(start, 2 * BLOCK_TOK), 2 * BLOCK_TOK)]

    def write_query(pair, value):
        start = rows + pl.multiple_of(pair % pairs_each * BLOCK_TOK, BLOCK_TOK)
        out_ref[pair // pairs_each, pl.ds(start, BLOCK_TOK)] = value.astype(jnp.bfloat16)

    for source in range(sources):
        part = slice((2 * source + 1) * rows, (2 * source + 2) * rows)
        swap_ref[part] = swap_halves(packed_ref[part])
    accumulate_blocks(
        sources * pairs_each,
        list_ref,
        place_ref,
        query_pair,
        lambda start: packed_ref[pl.ds(start, BLOCK_TOK)],
        lambda start: swap_ref[pl.ds(start, BLOCK_TOK)],
        write_query,
        acc_ref,
        buffers,
    )

    def write(source, carry):
        start = pl.multiple_of(source * rows, rows)
        out_ref[source, :rows] = (acc_ref[pl.ds(start, rows)] * key_scale()).astype(jnp.bfloat16)
        return carry

    lax.fori_loop(0, sources, write, 0)


def work_buffers():
    return [
        pltpu.VMEM((LIST_ROWS, 2 * PAIR), jnp.float32),
        pltpu.VMEM((SUBLANES, PAIR), jnp.float32),
    ] * 2


def listed_slots(block_slot, neighbours):
    slot_ids = jnp.arange(block_slot.shape[0], dtype=jnp.int32)
    matches = (block_slot[None, :] == slot_ids[:, None]).astype(jnp.int32)
    sphere_of = jnp.sum(matches * slot_ids[None, :], axis=1)
    return block_slot[neighbours[sphere_of]]


def one_head_each(queries, key_states, value_states, grad_output, block_slot, neighbours):
    axes = ("ctx", "head")
    rows, width = queries.shape
    heads = width // HEAD_DIM
    tokens = heads * rows
    in_vmem, in_smem = pltpu.VMEM, pltpu.SMEM
    packed = pl.pallas_call(
        pack_kernel,
        in_specs=[pl.BlockSpec(memory_space=pl.ANY)] * 4,
        out_specs=pl.BlockSpec(memory_space=pl.ANY),
        out_shape=jax.ShapeDtypeStruct((heads, 2, rows, PAIR), jnp.bfloat16),
        scratch_shapes=[
            pltpu.VMEM((4, rows, width), jnp.bfloat16),
            pltpu.VMEM((heads, 2, rows, PAIR), jnp.bfloat16),
            pltpu.SemaphoreType.DMA((4,)),
            pltpu.SemaphoreType.DMA((2, 2)),
        ],
        compiler_params=pltpu.CompilerParams(vmem_limit_bytes=PACK_VMEM_LIMIT),
    )(queries, grad_output, key_states, value_states)
    packed = lax.all_to_all(packed, axes, split_axis=0, concat_axis=0, tiled=True)
    place = listed_slots(block_slot, neighbours).reshape(-1) * BLOCK_TOK
    start = place // rows * (2 * rows) + rows + place % rows
    grads = call_kernel(
        head_kernel,
        jax.ShapeDtypeStruct((heads, 3 * rows // 2, PAIR), jnp.bfloat16),
        [in_smem, in_smem, in_vmem],
        [pltpu.VMEM((tokens, PAIR), jnp.float32), pltpu.VMEM((2 * tokens, PAIR), jnp.bfloat16)]
        + work_buffers(),
        flops=10 * tokens * LIST_ROWS * HEAD_DIM,
        bytes_accessed=7 * tokens * PAIR,
        transcendentals=tokens * LIST_ROWS,
    )(start, place, packed.reshape(2 * tokens, PAIR))
    grads = lax.all_to_all(grads, axes, split_axis=0, concat_axis=0, tiled=True)
    return pl.pallas_call(
        unpack_kernel,
        out_shape=(jax.ShapeDtypeStruct((rows, width), jnp.bfloat16),) * 3,
        in_specs=[pl.BlockSpec(memory_space=in_vmem)],
        out_specs=(pl.BlockSpec(memory_space=pl.ANY),) * 3,
        scratch_shapes=[pltpu.VMEM((3, rows, width), jnp.bfloat16), pltpu.SemaphoreType.DMA((3,))],
        compiler_params=pltpu.CompilerParams(vmem_limit_bytes=VMEM_LIMIT),
    )(grads)


def halo_kernel(list_ref, query_ref, key_value_ref, grad_query_out, acc_out, swap_ref, *buffers):
    for head in range(query_ref.shape[0]):
        swap_ref[...] = swap_halves(key_value_ref[head])

        def write_query(pair, value):
            grad_query_out[head, pl.ds(pl.multiple_of(pair * BLOCK_TOK, BLOCK_TOK), BLOCK_TOK)] = value

        accumulate_blocks(
            query_ref.shape[1] // (2 * BLOCK_TOK),
            list_ref,
            list_ref,
            lambda pair: query_ref[head, pl.ds(pl.multiple_of(pair * 2 * BLOCK_TOK, 2 * BLOCK_TOK), 2 * BLOCK_TOK)],
            lambda start: key_value_ref[head, pl.ds(start, BLOCK_TOK)],
            lambda start: swap_ref[pl.ds(start, BLOCK_TOK)],
            write_query,
            acc_out.at[head],
            buffers,
        )
        acc_out[head] = acc_out[head] * key_scale()


def halo_exchange(queries, key_states, value_states, grad_output, block_slot, neighbours):
    def to_heads(value):
        return lax.all_to_all(value, "head", split_axis=1, concat_axis=0, tiled=True)

    def paired(left, right):
        parts = [to_heads(x).reshape(-1, heads, 1, HEAD_DIM) for x in (left, right)]
        both = jnp.concatenate(parts, axis=2)
        return jnp.moveaxis(both, 1, 0).reshape(heads, -1, PAIR)

    heads = queries.shape[1] // HEAD_DIM // lax.axis_size("head")
    query_side = paired(queries, grad_output)
    key_side = paired(key_states, value_states)
    rows = query_side.shape[1]
    blocks = rows // BLOCK_TOK
    ctx_size = lax.axis_size("ctx")
    ctx_here = lax.axis_index("ctx")
    listed = lax.dynamic_slice_in_dim(listed_slots(block_slot, neighbours), ctx_here * blocks, blocks, 0)
    gap = (listed // blocks - ctx_here + ctx_size + REACH) % ctx_size - REACH
    lookup = (gap + REACH) * blocks + listed % blocks
    offsets = range(-REACH, REACH + 1)
    span = jnp.concatenate(
        [key_side if o == 0 else from_behind(key_side, "ctx", -o) for o in offsets], axis=1
    )
    grad_query, partial = call_kernel(
        halo_kernel,
        (
            jax.ShapeDtypeStruct((heads, rows // 2, PAIR), jnp.float32),
            jax.ShapeDtypeStruct(span.shape, jnp.float32),
        ),
        [pltpu.SMEM, pltpu.VMEM, pltpu.VMEM],
        [pltpu.VMEM(span.shape[1:], jnp.bfloat16)] + work_buffers(),
    )(lookup.reshape(-1) * BLOCK_TOK, query_side, span)
    returned = partial.reshape(heads, 2 * REACH + 1, rows, PAIR)
    summed = returned[:, REACH]
    for offset in offsets:
        if offset != 0:
            summed = summed + from_behind(returned[:, offset + REACH], "ctx", offset)

    def to_tokens(value):
        value = jnp.moveaxis(value.astype(jnp.bfloat16), 0, 1).reshape(rows, heads * HEAD_DIM)
        return lax.all_to_all(value, "head", split_axis=0, concat_axis=1, tiled=True)

    grad_query = grad_query.reshape(heads, blocks // 2, BLOCK_TOK, 2, HEAD_DIM)
    return (
        to_tokens(jnp.swapaxes(grad_query, 2, 3).reshape(heads, rows, HEAD_DIM)),
        to_tokens(summed[..., :HEAD_DIM]),
        to_tokens(summed[..., HEAD_DIM:]),
    )


def solution(mesh):
    devices = mesh.shape["ctx"] * mesh.shape["head"]

    def body(queries, *rest):
        rows, width = queries.shape
        one_each = width == devices * HEAD_DIM and rows % (4 * BLOCK_TOK) == 0
        return (one_head_each if one_each else halo_exchange)(queries, *rest)

    tokens = P(("band", "ctx", "head"), None)
    return jax.shard_map(
        body,
        mesh=mesh,
        in_specs=(tokens,) * 4 + (P("band"), P("band", None)),
        out_specs=(tokens,) * 3,
        check_vma=False,
    )
```

```python
import math

import jax
import jax.numpy as jnp
from jax import lax
from jax.experimental import pallas as pl
from jax.experimental.pallas import tpu as pltpu
from jax.sharding import PartitionSpec as P

HEAD_DIM = 64
BLOCK_TOK = 64
NBR = 8
REACH = 1
PAIR = 2 * HEAD_DIM
LIST_ROWS = NBR * BLOCK_TOK
SCALE = HEAD_DIM ** -0.5
EXP2_SCALE = SCALE * math.log2(math.e)
SUBLANES = 8
CHUNK = 32
VMEM_LIMIT = 48 * 1024 * 1024
PACK_VMEM_LIMIT = 60 * 1024 * 1024
NT = (((1,), (1,)), ((), ()))
NN = (((1,), (0,)), ((), ()))
TN = (((0,), (0,)), ((), ()))


def from_behind(value, axis, steps):
    count = lax.axis_size(axis)
    pairs = [(source, (source + steps) % count) for source in range(count)]
    return lax.ppermute(value, axis, pairs)


def call_kernel(kernel, out_shape, in_memory, scratch_shapes=(), **cost):
    outs = jax.tree.map(lambda _: pl.BlockSpec(memory_space=pltpu.VMEM), out_shape)
    return pl.pallas_call(
        kernel,
        out_shape=out_shape,
        in_specs=[pl.BlockSpec(memory_space=space) for space in in_memory],
        out_specs=outs,
        scratch_shapes=list(scratch_shapes),
        compiler_params=pltpu.CompilerParams(vmem_limit_bytes=VMEM_LIMIT),
        cost_estimate=pl.CostEstimate(**cost) if cost else None,
    )


def columns_of(ref, head):
    return ref[:, head * HEAD_DIM : (head + 1) * HEAD_DIM]


def pack_kernel(query_ref, grad_ref, key_ref, value_ref, out_ref):
    for head in range(out_ref.shape[0]):
        out_ref[head, 0] = jnp.concatenate([columns_of(query_ref, head), columns_of(grad_ref, head)], axis=1)
        out_ref[head, 1] = jnp.concatenate([columns_of(key_ref, head), columns_of(value_ref, head)], axis=1)


def unpack_kernel(packed_ref, query_ref, key_ref, value_ref, held, sems):
    rows, width = query_ref.shape
    heads = packed_ref.shape[0]

    def halves(pair, part, lanes):
        return jnp.concatenate([packed_ref[2 * pair, part, lanes], packed_ref[2 * pair + 1, part, lanes]], axis=1)

    def columns(pair):
        return slice(pair * PAIR, (pair + 1) * PAIR)

    copies = []
    first, second = slice(0, HEAD_DIM), slice(HEAD_DIM, PAIR)
    for n, (out_ref, lanes) in enumerate(((key_ref, first), (value_ref, second))):
        for pair in range(heads // 2):
            held[n, :, columns(pair)] = halves(pair, slice(0, rows), lanes)
        copies.append(pltpu.make_async_copy(held.at[n], out_ref, sems.at[n]))
        copies[-1].start()
    for place in range(rows // BLOCK_TOK):
        start = rows + place // 2 * BLOCK_TOK
        lanes = second if place % 2 else first
        for pair in range(heads // 2):
            held[2, place * BLOCK_TOK : (place + 1) * BLOCK_TOK, columns(pair)] = halves(
                pair, slice(start, start + BLOCK_TOK), lanes
            )
    copies.append(pltpu.make_async_copy(held.at[2], query_ref, sems.at[2]))
    copies[-1].start()
    for copy in copies:
        copy.wait()


def diagonal_of(rows):
    low = lax.broadcasted_iota(jnp.int32, (BLOCK_TOK, PAIR), 1) < HEAD_DIM
    rows_a, rows_b = rows[:BLOCK_TOK], rows[BLOCK_TOK:]
    zero = jnp.zeros_like(rows_a)
    return jnp.concatenate(
        [
            jnp.concatenate([jnp.where(low, rows_a, zero), zero], axis=1),
            jnp.concatenate([zero, jnp.where(low, rows_b, zero)], axis=1),
            jnp.concatenate([jnp.where(low, zero, rows_a), zero], axis=1),
            jnp.concatenate([zero, jnp.where(low, zero, rows_b)], axis=1),
        ],
        axis=0,
    )


def swap_halves(rows):
    return jnp.concatenate([rows[:, HEAD_DIM:], rows[:, :HEAD_DIM]], axis=1)


def fold_rows(value, reduce):
    return reduce(value.reshape(-1, SUBLANES, PAIR), axis=0)


def accumulate_blocks(
    pairs, list_ref, place_ref, query_pair, key_value_rows, value_key_rows, write_query, acc_ref, buffers
):
    count = 2 * NBR

    def listed_of(pair):
        starts = [pl.multiple_of(list_ref[pair * count + n], BLOCK_TOK) for n in range(count)]
        blocks = [key_value_rows(start) for start in starts]
        return jnp.concatenate(
            [jnp.concatenate(blocks[:NBR], axis=0), jnp.concatenate(blocks[NBR:], axis=0)], axis=1
        )

    def listed_keys(pair):
        low = lax.broadcasted_iota(jnp.int32, (BLOCK_TOK, PAIR), 1) < HEAD_DIM
        starts = [pl.multiple_of(list_ref[pair * count + n], BLOCK_TOK) for n in range(count)]
        return jnp.concatenate(
            [
                jnp.where(low, key_value_rows(starts[n]), value_key_rows(starts[NBR + n]))
                for n in range(NBR)
            ],
            axis=0,
        )

    def scores_stage(pair, buffer):
        both_ref, stat_ref = buffer
        both = lax.dot_general(
            listed_of(pair), diagonal_of(query_pair(pair)), NT, preferred_element_type=jnp.float32
        )
        both_ref[...] = both
        stat_ref[...] = fold_rows(both[:, :PAIR], jnp.max)

    def softmax_stage(buffer):
        both_ref, stat_ref = buffer
        top = jnp.max(stat_ref[...], axis=0, keepdims=True) * EXP2_SCALE
        total = delta = None
        for start in range(0, LIST_ROWS, CHUNK):
            rows = slice(start, start + CHUNK)
            weights = jnp.exp2(both_ref[rows, :PAIR] * EXP2_SCALE - top)
            part, part_delta = fold_rows(weights, jnp.sum), fold_rows(weights * both_ref[rows, PAIR:], jnp.sum)
            both_ref[rows, :PAIR] = weights
            total = part if total is None else total + part
            delta = part_delta if delta is None else delta + part_delta
        inverse = 1.0 / jnp.sum(total, axis=0, keepdims=True)
        stat_ref[0:1] = inverse
        stat_ref[1:2] = jnp.sum(delta, axis=0, keepdims=True) * inverse

    def gradients_stage(pair, buffer):
        both_ref, stat_ref = buffer
        inverse, row_delta = stat_ref[0:1], stat_ref[1:2]
        probability = both_ref[:, :PAIR] * inverse
        score_low = (probability * (both_ref[:, PAIR:] - row_delta)).astype(jnp.bfloat16)
        grad_listed = lax.dot_general(
            jnp.concatenate([score_low, probability.astype(jnp.bfloat16)], axis=1),
            diagonal_of(query_pair(pair)),
            NN,
            preferred_element_type=jnp.float32,
        )
        for n in range(NBR):
            for side in range(2):
                start = pl.multiple_of(place_ref[pair * count + side * NBR + n], BLOCK_TOK)
                acc_ref[pl.ds(start, BLOCK_TOK)] += grad_listed[
                    n * BLOCK_TOK : (n + 1) * BLOCK_TOK, side * PAIR : (side + 1) * PAIR
                ]
        grad_query = lax.dot_general(score_low, listed_keys(pair), TN, preferred_element_type=jnp.float32)
        low = lax.broadcasted_iota(jnp.int32, (BLOCK_TOK, PAIR), 1) < HEAD_DIM
        write_query(pair, jnp.where(low, grad_query[:BLOCK_TOK], grad_query[BLOCK_TOK:]) * SCALE)

    even, odd = buffers[:2], buffers[2:]
    acc_ref[...] = jnp.zeros_like(acc_ref)
    scores_stage(0, even)
    softmax_stage(even)
    scores_stage(1, odd)

    def step(index, carry):
        pair = 2 * index
        gradients_stage(pair, even)
        softmax_stage(odd)
        scores_stage(pair + 2, even)
        gradients_stage(pair + 1, odd)
        softmax_stage(even)
        scores_stage(pair + 3, odd)
        return carry

    lax.fori_loop(0, pairs // 2 - 1, step, 0)
    gradients_stage(pairs - 2, even)
    softmax_stage(odd)
    gradients_stage(pairs - 1, odd)


def key_scale():
    low = lax.broadcasted_iota(jnp.int32, (1, PAIR), 1) < HEAD_DIM
    return jnp.where(low, jnp.float32(SCALE), jnp.float32(1.0))


def head_kernel(list_ref, place_ref, packed_ref, out_ref, acc_ref, swap_ref, *buffers):
    sources, out_rows, _ = out_ref.shape
    rows = 2 * out_rows // 3
    pairs_each = rows // (2 * BLOCK_TOK)

    def query_pair(pair):
        start = pair // pairs_each * (2 * rows) + pair % pairs_each * (2 * BLOCK_TOK)
        return packed_ref[pl.ds(pl.multiple_of(start, 2 * BLOCK_TOK), 2 * BLOCK_TOK)]

    def write_query(pair, value):
        start = rows + pl.multiple_of(pair % pairs_each * BLOCK_TOK, BLOCK_TOK)
        out_ref[pair // pairs_each, pl.ds(start, BLOCK_TOK)] = value.astype(jnp.bfloat16)

    for source in range(sources):
        part = slice((2 * source + 1) * rows, (2 * source + 2) * rows)
        swap_ref[part] = swap_halves(packed_ref[part])
    accumulate_blocks(
        sources * pairs_each,
        list_ref,
        place_ref,
        query_pair,
        lambda start: packed_ref[pl.ds(start, BLOCK_TOK)],
        lambda start: swap_ref[pl.ds(start, BLOCK_TOK)],
        write_query,
        acc_ref,
        buffers,
    )

    def write(source, carry):
        start = pl.multiple_of(source * rows, rows)
        out_ref[source, :rows] = (acc_ref[pl.ds(start, rows)] * key_scale()).astype(jnp.bfloat16)
        return carry

    lax.fori_loop(0, sources, write, 0, unroll=4)


def work_buffers():
    return [
        pltpu.VMEM((LIST_ROWS, 2 * PAIR), jnp.float32),
        pltpu.VMEM((SUBLANES, PAIR), jnp.float32),
    ] * 2


def listed_slots(block_slot, neighbours):
    slot_ids = jnp.arange(block_slot.shape[0], dtype=jnp.int32)
    matches = (block_slot[None, :] == slot_ids[:, None]).astype(jnp.int32)
    sphere_of = jnp.sum(matches * slot_ids[None, :], axis=1)
    return block_slot[neighbours[sphere_of]]


def one_head_each(queries, key_states, value_states, grad_output, block_slot, neighbours):
    axes = ("ctx", "head")
    rows, width = queries.shape
    heads = width // HEAD_DIM
    tokens = heads * rows
    in_vmem, in_smem = pltpu.VMEM, pltpu.SMEM
    packed = pl.pallas_call(
        pack_kernel,
        grid=(2,),
        in_specs=[pl.BlockSpec((rows // 2, width), lambda i: (i, 0))] * 4,
        out_specs=pl.BlockSpec((heads, 2, rows // 2, PAIR), lambda i: (0, 0, i, 0)),
        out_shape=jax.ShapeDtypeStruct((heads, 2, rows, PAIR), jnp.bfloat16),
        compiler_params=pltpu.CompilerParams(vmem_limit_bytes=PACK_VMEM_LIMIT),
    )(queries, grad_output, key_states, value_states)
    packed = lax.all_to_all(packed, axes, split_axis=0, concat_axis=0, tiled=True)
    place = listed_slots(block_slot, neighbours).reshape(-1) * BLOCK_TOK
    start = place // rows * (2 * rows) + rows + place % rows
    grads = call_kernel(
        head_kernel,
        jax.ShapeDtypeStruct((heads, 3 * rows // 2, PAIR), jnp.bfloat16),
        [in_smem, in_smem, in_vmem],
        [pltpu.VMEM((tokens, PAIR), jnp.float32), pltpu.VMEM((2 * tokens, PAIR), jnp.bfloat16)]
        + work_buffers(),
        flops=10 * tokens * LIST_ROWS * HEAD_DIM,
        bytes_accessed=7 * tokens * PAIR,
        transcendentals=tokens * LIST_ROWS,
    )(start, place, packed.reshape(2 * tokens, PAIR))
    grads = lax.all_to_all(grads, axes, split_axis=0, concat_axis=0, tiled=True)
    return pl.pallas_call(
        unpack_kernel,
        out_shape=(jax.ShapeDtypeStruct((rows, width), jnp.bfloat16),) * 3,
        in_specs=[pl.BlockSpec(memory_space=in_vmem)],
        out_specs=(pl.BlockSpec(memory_space=pl.ANY),) * 3,
        scratch_shapes=[pltpu.VMEM((3, rows, width), jnp.bfloat16), pltpu.SemaphoreType.DMA((3,))],
        compiler_params=pltpu.CompilerParams(vmem_limit_bytes=VMEM_LIMIT),
    )(grads)


def halo_kernel(list_ref, query_ref, key_value_ref, grad_query_out, acc_out, swap_ref, *buffers):
    for head in range(query_ref.shape[0]):
        swap_ref[...] = swap_halves(key_value_ref[head])

        def write_query(pair, value):
            grad_query_out[head, pl.ds(pl.multiple_of(pair * BLOCK_TOK, BLOCK_TOK), BLOCK_TOK)] = value

        accumulate_blocks(
            query_ref.shape[1] // (2 * BLOCK_TOK),
            list_ref,
            list_ref,
            lambda pair: query_ref[head, pl.ds(pl.multiple_of(pair * 2 * BLOCK_TOK, 2 * BLOCK_TOK), 2 * BLOCK_TOK)],
            lambda start: key_value_ref[head, pl.ds(start, BLOCK_TOK)],
            lambda start: swap_ref[pl.ds(start, BLOCK_TOK)],
            write_query,
            acc_out.at[head],
            buffers,
        )
        acc_out[head] = acc_out[head] * key_scale()


def halo_exchange(queries, key_states, value_states, grad_output, block_slot, neighbours):
    def to_heads(value):
        return lax.all_to_all(value, "head", split_axis=1, concat_axis=0, tiled=True)

    def paired(left, right):
        parts = [to_heads(x).reshape(-1, heads, 1, HEAD_DIM) for x in (left, right)]
        both = jnp.concatenate(parts, axis=2)
        return jnp.moveaxis(both, 1, 0).reshape(heads, -1, PAIR)

    heads = queries.shape[1] // HEAD_DIM // lax.axis_size("head")
    query_side = paired(queries, grad_output)
    key_side = paired(key_states, value_states)
    rows = query_side.shape[1]
    blocks = rows // BLOCK_TOK
    ctx_size = lax.axis_size("ctx")
    ctx_here = lax.axis_index("ctx")
    listed = lax.dynamic_slice_in_dim(listed_slots(block_slot, neighbours), ctx_here * blocks, blocks, 0)
    gap = (listed // blocks - ctx_here + ctx_size + REACH) % ctx_size - REACH
    lookup = (gap + REACH) * blocks + listed % blocks
    offsets = range(-REACH, REACH + 1)
    span = jnp.concatenate(
        [key_side if o == 0 else from_behind(key_side, "ctx", -o) for o in offsets], axis=1
    )
    grad_query, partial = call_kernel(
        halo_kernel,
        (
            jax.ShapeDtypeStruct((heads, rows // 2, PAIR), jnp.float32),
            jax.ShapeDtypeStruct(span.shape, jnp.float32),
        ),
        [pltpu.SMEM, pltpu.VMEM, pltpu.VMEM],
        [pltpu.VMEM(span.shape[1:], jnp.bfloat16)] + work_buffers(),
    )(lookup.reshape(-1) * BLOCK_TOK, query_side, span)
    returned = partial.reshape(heads, 2 * REACH + 1, rows, PAIR)
    summed = returned[:, REACH]
    for offset in offsets:
        if offset != 0:
            summed = summed + from_behind(returned[:, offset + REACH], "ctx", offset)

    def to_tokens(value):
        value = jnp.moveaxis(value.astype(jnp.bfloat16), 0, 1).reshape(rows, heads * HEAD_DIM)
        return lax.all_to_all(value, "head", split_axis=0, concat_axis=1, tiled=True)

    grad_query = grad_query.reshape(heads, blocks // 2, BLOCK_TOK, 2, HEAD_DIM)
    return (
        to_tokens(jnp.swapaxes(grad_query, 2, 3).reshape(heads, rows, HEAD_DIM)),
        to_tokens(summed[..., :HEAD_DIM]),
        to_tokens(summed[..., HEAD_DIM:]),
    )


def solution(mesh):
    devices = mesh.shape["ctx"] * mesh.shape["head"]

    def body(queries, *rest):
        rows, width = queries.shape
        one_each = width == devices * HEAD_DIM and rows % (4 * BLOCK_TOK) == 0
        return (one_head_each if one_each else halo_exchange)(queries, *rest)

    tokens = P(("band", "ctx", "head"), None)
    return jax.shard_map(
        body,
        mesh=mesh,
        in_specs=(tokens,) * 4 + (P("band"), P("band", None)),
        out_specs=(tokens,) * 3,
        check_vma=False,
    )
```

```python
import math

import jax
import jax.numpy as jnp
from jax import lax
from jax.experimental import pallas as pl
from jax.experimental.pallas import tpu as pltpu
from jax.sharding import PartitionSpec as P

HEAD_DIM = 64
BLOCK_TOK = 64
NBR = 8
REACH = 1
PAIR = 2 * HEAD_DIM
LIST_ROWS = NBR * BLOCK_TOK
SCALE = HEAD_DIM ** -0.5
EXP2_SCALE = SCALE * math.log2(math.e)
SUBLANES = 8
CHUNK = 16
VMEM_LIMIT = 48 * 1024 * 1024
PACK_VMEM_LIMIT = 60 * 1024 * 1024
NT = (((1,), (1,)), ((), ()))
NN = (((1,), (0,)), ((), ()))
TN = (((0,), (0,)), ((), ()))


def from_behind(value, axis, steps):
    count = lax.axis_size(axis)
    pairs = [(source, (source + steps) % count) for source in range(count)]
    return lax.ppermute(value, axis, pairs)


def call_kernel(kernel, out_shape, in_memory, scratch_shapes=(), **cost):
    outs = jax.tree.map(lambda _: pl.BlockSpec(memory_space=pltpu.VMEM), out_shape)
    return pl.pallas_call(
        kernel,
        out_shape=out_shape,
        in_specs=[pl.BlockSpec(memory_space=space) for space in in_memory],
        out_specs=outs,
        scratch_shapes=list(scratch_shapes),
        compiler_params=pltpu.CompilerParams(vmem_limit_bytes=VMEM_LIMIT),
        cost_estimate=pl.CostEstimate(**cost) if cost else None,
    )


def columns_of(ref, head):
    return ref[:, head * HEAD_DIM : (head + 1) * HEAD_DIM]


def pack_kernel(query_ref, grad_ref, key_ref, value_ref, out_ref, held, ready, in_sems, out_sems):
    heads = out_ref.shape[0]
    groups = out_sems.shape[1]
    some = heads // groups
    arrays = (query_ref, grad_ref, key_ref, value_ref)
    loads = [pltpu.make_async_copy(array, held.at[n], in_sems.at[n]) for n, array in enumerate(arrays)]
    for load in loads:
        load.start()
    stores = []
    for kind in range(2):
        left, right = 2 * kind, 2 * kind + 1
        loads[left].wait()
        loads[right].wait()
        for group in range(groups):
            for head in range(group * some, (group + 1) * some):
                ready[head, kind] = jnp.concatenate(
                    [columns_of(held.at[left], head), columns_of(held.at[right], head)], axis=1
                )
            part = pl.ds(group * some, some)
            stores.append(
                pltpu.make_async_copy(ready.at[part, kind], out_ref.at[part, kind], out_sems.at[kind, group])
            )
            stores[-1].start()
    for store in stores:
        store.wait()


def unpack_kernel(packed_ref, query_ref, key_ref, value_ref, held, sems):
    rows, width = query_ref.shape
    heads = packed_ref.shape[0]

    def halves(pair, part, lanes):
        return jnp.concatenate([packed_ref[2 * pair, part, lanes], packed_ref[2 * pair + 1, part, lanes]], axis=1)

    def columns(pair):
        return slice(pair * PAIR, (pair + 1) * PAIR)

    copies = []
    first, second = slice(0, HEAD_DIM), slice(HEAD_DIM, PAIR)
    for n, (out_ref, lanes) in enumerate(((key_ref, first), (value_ref, second))):
        for pair in range(heads // 2):
            held[n, :, columns(pair)] = halves(pair, slice(0, rows), lanes)
        copies.append(pltpu.make_async_copy(held.at[n], out_ref, sems.at[n]))
        copies[-1].start()
    for place in range(rows // BLOCK_TOK):
        start = rows + place // 2 * BLOCK_TOK
        lanes = second if place % 2 else first
        for pair in range(heads // 2):
            held[2, place * BLOCK_TOK : (place + 1) * BLOCK_TOK, columns(pair)] = halves(
                pair, slice(start, start + BLOCK_TOK), lanes
            )
    copies.append(pltpu.make_async_copy(held.at[2], query_ref, sems.at[2]))
    copies[-1].start()
    for copy in copies:
        copy.wait()


def diagonal_of(rows):
    low = lax.broadcasted_iota(jnp.int32, (BLOCK_TOK, PAIR), 1) < HEAD_DIM
    rows_a, rows_b = rows[:BLOCK_TOK], rows[BLOCK_TOK:]
    zero = jnp.zeros_like(rows_a)
    return jnp.concatenate(
        [
            jnp.concatenate([jnp.where(low, rows_a, zero), zero], axis=1),
            jnp.concatenate([zero, jnp.where(low, rows_b, zero)], axis=1),
            jnp.concatenate([jnp.where(low, zero, rows_a), zero], axis=1),
            jnp.concatenate([zero, jnp.where(low, zero, rows_b)], axis=1),
        ],
        axis=0,
    )


def swap_halves(rows):
    return jnp.concatenate([rows[:, HEAD_DIM:], rows[:, :HEAD_DIM]], axis=1)


def fold_rows(value, reduce):
    return reduce(value.reshape(-1, SUBLANES, PAIR), axis=0)


def accumulate_blocks(
    pairs, list_ref, place_ref, query_pair, key_value_rows, value_key_rows, write_query, acc_ref, buffers
):
    count = 2 * NBR

    def listed_of(pair):
        starts = [pl.multiple_of(list_ref[pair * count + n], BLOCK_TOK) for n in range(count)]
        blocks = [key_value_rows(start) for start in starts]
        return jnp.concatenate(
            [jnp.concatenate(blocks[:NBR], axis=0), jnp.concatenate(blocks[NBR:], axis=0)], axis=1
        )

    def listed_keys(pair):
        low = lax.broadcasted_iota(jnp.int32, (BLOCK_TOK, PAIR), 1) < HEAD_DIM
        starts = [pl.multiple_of(list_ref[pair * count + n], BLOCK_TOK) for n in range(count)]
        return jnp.concatenate(
            [
                jnp.where(low, key_value_rows(starts[n]), value_key_rows(starts[NBR + n]))
                for n in range(NBR)
            ],
            axis=0,
        )

    def scores_stage(pair, buffer):
        both_ref, stat_ref = buffer
        both = lax.dot_general(
            listed_of(pair), diagonal_of(query_pair(pair)), NT, preferred_element_type=jnp.float32
        )
        both_ref[...] = both
        stat_ref[...] = fold_rows(both[:, :PAIR], jnp.max)

    def softmax_stage(buffer):
        both_ref, stat_ref = buffer
        top = jnp.max(stat_ref[...], axis=0, keepdims=True) * EXP2_SCALE
        total = delta = None
        for start in range(0, LIST_ROWS, CHUNK):
            rows = slice(start, start + CHUNK)
            weights = jnp.exp2(both_ref[rows, :PAIR] * EXP2_SCALE - top)
            part, part_delta = fold_rows(weights, jnp.sum), fold_rows(weights * both_ref[rows, PAIR:], jnp.sum)
            both_ref[rows, :PAIR] = weights
            total = part if total is None else total + part
            delta = part_delta if delta is None else delta + part_delta
        inverse = 1.0 / jnp.sum(total, axis=0, keepdims=True)
        stat_ref[0:1] = inverse
        stat_ref[1:2] = jnp.sum(delta, axis=0, keepdims=True) * inverse

    def gradients_stage(pair, buffer):
        both_ref, stat_ref = buffer
        inverse, row_delta = stat_ref[0:1], stat_ref[1:2]
        probability = both_ref[:, :PAIR] * inverse
        score_low = (probability * (both_ref[:, PAIR:] - row_delta)).astype(jnp.bfloat16)
        grad_listed = lax.dot_general(
            jnp.concatenate([score_low, probability.astype(jnp.bfloat16)], axis=1),
            diagonal_of(query_pair(pair)),
            NN,
            preferred_element_type=jnp.float32,
        )
        for n in range(NBR):
            for side in range(2):
                start = pl.multiple_of(place_ref[pair * count + side * NBR + n], BLOCK_TOK)
                acc_ref[pl.ds(start, BLOCK_TOK)] += grad_listed[
                    n * BLOCK_TOK : (n + 1) * BLOCK_TOK, side * PAIR : (side + 1) * PAIR
                ]
        grad_query = lax.dot_general(score_low, listed_keys(pair), TN, preferred_element_type=jnp.float32)
        low = lax.broadcasted_iota(jnp.int32, (BLOCK_TOK, PAIR), 1) < HEAD_DIM
        write_query(pair, jnp.where(low, grad_query[:BLOCK_TOK], grad_query[BLOCK_TOK:]) * SCALE)

    even, odd = buffers[:2], buffers[2:]
    acc_ref[...] = jnp.zeros_like(acc_ref)
    scores_stage(0, even)
    softmax_stage(even)
    scores_stage(1, odd)

    def step(index, carry):
        pair = 2 * index
        gradients_stage(pair, even)
        softmax_stage(odd)
        scores_stage(pair + 2, even)
        gradients_stage(pair + 1, odd)
        softmax_stage(even)
        scores_stage(pair + 3, odd)
        return carry

    lax.fori_loop(0, pairs // 2 - 1, step, 0)
    gradients_stage(pairs - 2, even)
    softmax_stage(odd)
    gradients_stage(pairs - 1, odd)


def key_scale():
    low = lax.broadcasted_iota(jnp.int32, (1, PAIR), 1) < HEAD_DIM
    return jnp.where(low, jnp.float32(SCALE), jnp.float32(1.0))


def head_kernel(list_ref, place_ref, packed_ref, out_ref, acc_ref, swap_ref, *buffers):
    sources, out_rows, _ = out_ref.shape
    rows = 2 * out_rows // 3
    pairs_each = rows // (2 * BLOCK_TOK)

    def query_pair(pair):
        start = pair // pairs_each * (2 * rows) + pair % pairs_each * (2 * BLOCK_TOK)
        return packed_ref[pl.ds(pl.multiple_of(start, 2 * BLOCK_TOK), 2 * BLOCK_TOK)]

    def write_query(pair, value):
        start = rows + pl.multiple_of(pair % pairs_each * BLOCK_TOK, BLOCK_TOK)
        out_ref[pair // pairs_each, pl.ds(start, BLOCK_TOK)] = value.astype(jnp.bfloat16)

    for source in range(sources):
        part = slice((2 * source + 1) * rows, (2 * source + 2) * rows)
        swap_ref[part] = swap_halves(packed_ref[part])
    accumulate_blocks(
        sources * pairs_each,
        list_ref,
        place_ref,
        query_pair,
        lambda start: packed_ref[pl.ds(start, BLOCK_TOK)],
        lambda start: swap_ref[pl.ds(start, BLOCK_TOK)],
        write_query,
        acc_ref,
        buffers,
    )

    def write(source, carry):
        start = pl.multiple_of(source * rows, rows)
        out_ref[source, :rows] = (acc_ref[pl.ds(start, rows)] * key_scale()).astype(jnp.bfloat16)
        return carry

    lax.fori_loop(0, sources, write, 0, unroll=4)


def work_buffers():
    return [
        pltpu.VMEM((LIST_ROWS, 2 * PAIR), jnp.float32),
        pltpu.VMEM((SUBLANES, PAIR), jnp.float32),
    ] * 2


def listed_slots(block_slot, neighbours):
    slot_ids = jnp.arange(block_slot.shape[0], dtype=jnp.int32)
    matches = (block_slot[None, :] == slot_ids[:, None]).astype(jnp.int32)
    sphere_of = jnp.sum(matches * slot_ids[None, :], axis=1)
    return block_slot[neighbours[sphere_of]]


def one_head_each(queries, key_states, value_states, grad_output, block_slot, neighbours):
    axes = ("ctx", "head")
    rows, width = queries.shape
    heads = width // HEAD_DIM
    tokens = heads * rows
    in_vmem, in_smem = pltpu.VMEM, pltpu.SMEM
    packed = pl.pallas_call(
        pack_kernel,
        in_specs=[pl.BlockSpec(memory_space=pl.ANY)] * 4,
        out_specs=pl.BlockSpec(memory_space=pl.ANY),
        out_shape=jax.ShapeDtypeStruct((heads, 2, rows, PAIR), jnp.bfloat16),
        scratch_shapes=[
            pltpu.VMEM((4, rows, width), jnp.bfloat16),
            pltpu.VMEM((heads, 2, rows, PAIR), jnp.bfloat16),
            pltpu.SemaphoreType.DMA((4,)),
            pltpu.SemaphoreType.DMA((2, 2)),
        ],
        compiler_params=pltpu.CompilerParams(vmem_limit_bytes=PACK_VMEM_LIMIT),
    )(queries, grad_output, key_states, value_states)
    packed = lax.all_to_all(packed, axes, split_axis=0, concat_axis=0, tiled=True)
    place = listed_slots(block_slot, neighbours).reshape(-1) * BLOCK_TOK
    start = place // rows * (2 * rows) + rows + place % rows
    grads = call_kernel(
        head_kernel,
        jax.ShapeDtypeStruct((heads, 3 * rows // 2, PAIR), jnp.bfloat16),
        [in_smem, in_smem, in_vmem],
        [pltpu.VMEM((tokens, PAIR), jnp.float32), pltpu.VMEM((2 * tokens, PAIR), jnp.bfloat16)]
        + work_buffers(),
        flops=10 * tokens * LIST_ROWS * HEAD_DIM,
        bytes_accessed=7 * tokens * PAIR,
        transcendentals=tokens * LIST_ROWS,
    )(start, place, packed.reshape(2 * tokens, PAIR))
    grads = lax.all_to_all(grads, axes, split_axis=0, concat_axis=0, tiled=True)
    return pl.pallas_call(
        unpack_kernel,
        out_shape=(jax.ShapeDtypeStruct((rows, width), jnp.bfloat16),) * 3,
        in_specs=[pl.BlockSpec(memory_space=in_vmem)],
        out_specs=(pl.BlockSpec(memory_space=pl.ANY),) * 3,
        scratch_shapes=[pltpu.VMEM((3, rows, width), jnp.bfloat16), pltpu.SemaphoreType.DMA((3,))],
        compiler_params=pltpu.CompilerParams(vmem_limit_bytes=VMEM_LIMIT),
    )(grads)


def halo_kernel(list_ref, query_ref, key_value_ref, grad_query_out, acc_out, swap_ref, *buffers):
    for head in range(query_ref.shape[0]):
        swap_ref[...] = swap_halves(key_value_ref[head])

        def write_query(pair, value):
            grad_query_out[head, pl.ds(pl.multiple_of(pair * BLOCK_TOK, BLOCK_TOK), BLOCK_TOK)] = value

        accumulate_blocks(
            query_ref.shape[1] // (2 * BLOCK_TOK),
            list_ref,
            list_ref,
            lambda pair: query_ref[head, pl.ds(pl.multiple_of(pair * 2 * BLOCK_TOK, 2 * BLOCK_TOK), 2 * BLOCK_TOK)],
            lambda start: key_value_ref[head, pl.ds(start, BLOCK_TOK)],
            lambda start: swap_ref[pl.ds(start, BLOCK_TOK)],
            write_query,
            acc_out.at[head],
            buffers,
        )
        acc_out[head] = acc_out[head] * key_scale()


def halo_exchange(queries, key_states, value_states, grad_output, block_slot, neighbours):
    def to_heads(value):
        return lax.all_to_all(value, "head", split_axis=1, concat_axis=0, tiled=True)

    def paired(left, right):
        parts = [to_heads(x).reshape(-1, heads, 1, HEAD_DIM) for x in (left, right)]
        both = jnp.concatenate(parts, axis=2)
        return jnp.moveaxis(both, 1, 0).reshape(heads, -1, PAIR)

    heads = queries.shape[1] // HEAD_DIM // lax.axis_size("head")
    query_side = paired(queries, grad_output)
    key_side = paired(key_states, value_states)
    rows = query_side.shape[1]
    blocks = rows // BLOCK_TOK
    ctx_size = lax.axis_size("ctx")
    ctx_here = lax.axis_index("ctx")
    listed = lax.dynamic_slice_in_dim(listed_slots(block_slot, neighbours), ctx_here * blocks, blocks, 0)
    gap = (listed // blocks - ctx_here + ctx_size + REACH) % ctx_size - REACH
    lookup = (gap + REACH) * blocks + listed % blocks
    offsets = range(-REACH, REACH + 1)
    span = jnp.concatenate(
        [key_side if o == 0 else from_behind(key_side, "ctx", -o) for o in offsets], axis=1
    )
    grad_query, partial = call_kernel(
        halo_kernel,
        (
            jax.ShapeDtypeStruct((heads, rows // 2, PAIR), jnp.float32),
            jax.ShapeDtypeStruct(span.shape, jnp.float32),
        ),
        [pltpu.SMEM, pltpu.VMEM, pltpu.VMEM],
        [pltpu.VMEM(span.shape[1:], jnp.bfloat16)] + work_buffers(),
    )(lookup.reshape(-1) * BLOCK_TOK, query_side, span)
    returned = partial.reshape(heads, 2 * REACH + 1, rows, PAIR)
    summed = returned[:, REACH]
    for offset in offsets:
        if offset != 0:
            summed = summed + from_behind(returned[:, offset + REACH], "ctx", offset)

    def to_tokens(value):
        value = jnp.moveaxis(value.astype(jnp.bfloat16), 0, 1).reshape(rows, heads * HEAD_DIM)
        return lax.all_to_all(value, "head", split_axis=0, concat_axis=1, tiled=True)

    grad_query = grad_query.reshape(heads, blocks // 2, BLOCK_TOK, 2, HEAD_DIM)
    return (
        to_tokens(jnp.swapaxes(grad_query, 2, 3).reshape(heads, rows, HEAD_DIM)),
        to_tokens(summed[..., :HEAD_DIM]),
        to_tokens(summed[..., HEAD_DIM:]),
    )


def solution(mesh):
    devices = mesh.shape["ctx"] * mesh.shape["head"]

    def body(queries, *rest):
        rows, width = queries.shape
        one_each = width == devices * HEAD_DIM and rows % (4 * BLOCK_TOK) == 0
        return (one_head_each if one_each else halo_exchange)(queries, *rest)

    tokens = P(("band", "ctx", "head"), None)
    return jax.shard_map(
        body,
        mesh=mesh,
        in_specs=(tokens,) * 4 + (P("band"), P("band", None)),
        out_specs=(tokens,) * 3,
        check_vma=False,
    )
```
